512 devices in a mesh: mem: 64 (over z, x, core), dec: 8 (over y).
Axes of the slice: x: 4, y: 8, z: 8, core: 2. Of those that a mesh axis runs over, the one named last changes fastest.
Arguments:
- question_states: bfloat16 [64, 8, 4096], P('mem', None, 'dec'), may hold values from -6 to 6
- passage_cache: bfloat16 [256, 64, 4096], P('mem', None, 'dec'), may hold values from -6 to 6
- norm_gain: float32 [4096], replicated, may hold values from 0.1 to 1.9
- enc_wq: bfloat16 [4096, 2048], P('mem', 'dec'), may hold values from -0.09375 to 0.09375
- enc_wk: bfloat16 [4096, 2048], P('mem', 'dec'), may hold values from -0.09375 to 0.09375
- enc_wv: bfloat16 [4096, 2048], P('mem', 'dec'), may hold values from -0.09375 to 0.09375
- enc_wo: bfloat16 [2048, 4096], P('dec', 'mem'), may hold values from -0.125 to 0.125
- dec_wk: bfloat16 [4096, 2048], P('dec'), may hold values from -0.09375 to 0.09375
- dec_wv: bfloat16 [4096, 2048], P('dec'), may hold values from -0.09375 to 0.09375
- dec_queries: bfloat16 [64, 8, 2048], P('mem', None, 'dec'), may hold values from -6 to 6
- passage_ids: int32 [64, 2], replicated, may hold values from 0 to 255, as said below
- location: int32 [256], replicated, may hold values from 0 to 255, as said below
- question_lengths: int32 [64], replicated, may hold values from 1 to 8
Outputs:
- decoder_context: bfloat16 [64, 8, 2048], P('mem', None, 'dec')
The draws below stay inside these ranges and needn't reach their ends.
Inputs may be any that keep to these rules, and one draw needn't show every extreme that they name: `passage_ids`: the requests whose passage lies in cache rows s * 4 to (s + 1) * 4 - 1 number at most 3 for every s, and exactly 3 for some s; a question's passages need not differ. A permutation: passage p's states are row location[p] of passage_cache.
All inputs are finite; a program needn't handle non-finite values.
Results may differ from the reference program's by a relative error of at most 0.04.
Values may be sent and summed in bfloat16 or wider, within the bound.
A program may use at most 64 MiB of HBM per device.

```python
import jax
import jax.numpy as jnp
from jax import lax

D = 4096
HEADS = 32
HEAD_DIM = 64
P_SIZE = 64
QL = 8
KPASS = 2
ANS = 8
NP_DEV = 4
HD = 2048
Q = 64
NPASS = 256
N_DEC = 8


def shared_layout(key):
    location = jax.random.permutation(jax.random.fold_in(key, 11), NPASS).astype(jnp.int32)
    count_table = jnp.array([[3, 3, 2, 0], [3, 2, 2, 1], [3, 3, 1, 1], [2, 2, 2, 2], [1, 2, 2, 3], [0, 2, 3, 3]], jnp.int32)
    pattern_pick = jax.random.randint(jax.random.fold_in(key, 12), (Q // 4,), 0, 6)
    pattern_pick = pattern_pick.at[0].set(0)
    ranked_counts = count_table[pattern_pick].reshape(-1)
    owner_order = jax.random.permutation(jax.random.fold_in(key, 13), Q)
    counts = jnp.zeros((Q,), jnp.int32).at[owner_order].set(ranked_counts)
    request_total = Q * KPASS
    bounds = jnp.cumsum(counts)
    request_owner = jnp.sum((bounds[None, :] <= jnp.arange(request_total)[:, None]).astype(jnp.int32), axis=1)
    shuffled = jax.random.permutation(jax.random.fold_in(key, 14), request_total)
    request_owner = request_owner[shuffled]
    slot_pick = jax.random.randint(jax.random.fold_in(key, 15), (request_total,), 0, NP_DEV)
    cache_row = request_owner * NP_DEV + slot_pick
    inverse = jnp.argsort(location)
    passage_ids = inverse[cache_row].reshape(Q, KPASS).astype(jnp.int32)
    return (location, passage_ids)


def draw_location(key, part):
    return shared_layout(key)[0]


def draw_passage_ids(key, part):
    return shared_layout(key)[1]


def touch_ends(values, own_key, least, top_value):
    longest = values.shape.index(max(values.shape))
    spots = []
    for shift in (0, 1):
        where = [jax.random.randint(jax.random.fold_in(own_key, axis), (), 0, length) for axis, length in enumerate(values.shape)]
        where[longest] = (where[longest] + shift) % values.shape[longest]
        spots.append(tuple(where))
    return values.at[spots[0]].set(least).at[spots[1]].set(top_value)


def levels(rng, dims, pieces, low, largest):
    gain, own = 1.0, jax.random.fold_in(rng, 6)
    for dim, shards_of in pieces:
        heights = jnp.exp(jax.random.uniform(jax.random.fold_in(own, dim), (shards_of,), jnp.float32, low / len(pieces), largest / len(pieces)))
        gain = gain * jnp.repeat(heights, dims[dim] // shards_of).reshape([-1 if axis == dim else 1 for axis in range(len(dims))])
    return gain


def normal_values(rng, shape, deviation, bound, shards=(), kind=jnp.bfloat16):
    values = deviation * jax.random.normal(rng, shape, jnp.float32)
    if shards:
        values = values * levels(rng, shape, shards, -0.22, 0.18)
    return jnp.clip(values, -bound, bound).astype(kind)


def setup_inputs(seed: int = 0) -> dict:
    arg_keys = jax.random.split(jax.random.key(seed), 14)
    return {
        "question_states": normal_values(arg_keys[0], (Q, QL, D), 1.0, 6.0, ((0, 64), (2, 8))),
        "passage_cache": normal_values(arg_keys[1], (NPASS, P_SIZE, D), 1.0, 6.0, ((0, 64), (2, 8))),
        "norm_gain": jnp.clip(1.0 + 0.18 * jax.random.normal(arg_keys[2], (D,), jnp.float32), 0.1, 1.9),
        "enc_wq": normal_values(arg_keys[3], (D, HD), D ** -0.5, 0.09375, ((0, 64), (1, 8))),
        "enc_wk": normal_values(arg_keys[4], (D, HD), D ** -0.5, 0.09375, ((0, 64), (1, 8))),
        "enc_wv": normal_values(arg_keys[5], (D, HD), D ** -0.5, 0.09375, ((0, 64), (1, 8))),
        "enc_wo": normal_values(arg_keys[6], (HD, D), HD ** -0.5, 0.125, ((0, 8), (1, 64))),
        "dec_wk": normal_values(arg_keys[7], (D, HD), D ** -0.5, 0.09375, ((0, 8),)),
        "dec_wv": normal_values(arg_keys[8], (D, HD), D ** -0.5, 0.09375, ((0, 8),)),
        "dec_queries": normal_values(arg_keys[9], (Q, ANS, HD), 1.0, 6.0, ((0, 64), (2, 8))),
        "passage_ids": draw_passage_ids(jax.random.fold_in(arg_keys[13], 71), 0),
        "location": draw_location(jax.random.fold_in(arg_keys[13], 71), 0),
        "question_lengths": touch_ends(jax.random.randint(arg_keys[12], (Q,), 1, QL + 1), jax.random.fold_in(arg_keys[12], 1), 1, QL).astype(jnp.int32),
    }


NORM_EPSILON = 1e-06

def rounded(value):
    return lax.optimization_barrier(value.astype(jnp.bfloat16))

def reference(question_states, passage_cache, norm_gain, enc_wq, enc_wk, enc_wv, enc_wo, dec_wk, dec_wv, dec_queries, passage_ids, location, question_lengths):
    hd_total = HEADS * HEAD_DIM
    pair_rows = QL + P_SIZE
    group_heads = hd_total // N_DEC
    group_width = D // N_DEC
    score_scale = HEAD_DIM ** (-0.5)
    positions = jnp.arange(pair_rows)

    def one_question(question_index):
        cache_rows = location[passage_ids[question_index]]
        passages = passage_cache[cache_rows]
        own_states = jnp.broadcast_to(question_states[question_index][None], (KPASS, QL, D))
        widened = jnp.concatenate([own_states, passages], axis=1).astype(jnp.float32)
        squares = lax.optimization_barrier(jnp.mean(widened * widened, axis=2, keepdims=True))
        normed = rounded(widened * lax.rsqrt(squares + NORM_EPSILON) * norm_gain).reshape(KPASS * pair_rows, D)
        shape_four = (KPASS, pair_rows, HEADS, HEAD_DIM)
        queries = rounded(jnp.dot(normed, enc_wq, preferred_element_type=jnp.float32)).astype(jnp.float32).reshape(shape_four)
        enc_keys = rounded(jnp.dot(normed, enc_wk, preferred_element_type=jnp.float32)).astype(jnp.float32).reshape(shape_four)
        enc_values = rounded(jnp.dot(normed, enc_wv, preferred_element_type=jnp.float32)).astype(jnp.float32).reshape(shape_four)
        live_keys = ((positions >= QL) | (positions < question_lengths[question_index])).astype(jnp.float32)
        scores = jnp.einsum('cihe,cjhe->chij', queries, enc_keys) * score_scale
        weights = jnp.exp(scores) * live_keys[None, None, None, :]
        probabilities = rounded(weights / lax.optimization_barrier(jnp.sum(weights, axis=3, keepdims=True))).astype(jnp.float32)
        context = rounded(jnp.einsum('chij,cjhe->cihe', probabilities, enc_values)).reshape(KPASS * pair_rows, hd_total)
        attended = jnp.zeros((KPASS * pair_rows, D), jnp.float32)
        for group_index in range(N_DEC):
            low = group_index * group_heads
            group_part = jnp.dot(context[:, low:low + group_heads], enc_wo[low:low + group_heads], preferred_element_type=jnp.float32)
            attended = attended + rounded(group_part).astype(jnp.float32)
        encoded = rounded(widened.reshape(KPASS * pair_rows, D) + attended)
        key_sum = jnp.zeros((KPASS * pair_rows, hd_total), jnp.float32)
        value_sum = jnp.zeros((KPASS * pair_rows, hd_total), jnp.float32)
        for group_index in range(N_DEC):
            low = group_index * group_width
            block = encoded[:, low:low + group_width]
            key_sum = key_sum + rounded(jnp.dot(block, dec_wk[low:low + group_width], preferred_element_type=jnp.float32)).astype(jnp.float32)
            value_sum = value_sum + rounded(jnp.dot(block, dec_wv[low:low + group_width], preferred_element_type=jnp.float32)).astype(jnp.float32)
        dec_keys = rounded(key_sum).astype(jnp.float32).reshape(shape_four)
        dec_values = rounded(value_sum).astype(jnp.float32).reshape(shape_four)
        asked = dec_queries[question_index].astype(jnp.float32).reshape(ANS, HEADS, HEAD_DIM)
        cross_scores = jnp.einsum('ahe,cjhe->hacj', asked, dec_keys) * score_scale
        cross_weight = jnp.exp(cross_scores) * live_keys[None, None, None, :]
        numerators = jnp.einsum('hacj,cjhe->ahe', rounded(cross_weight).astype(jnp.float32), dec_values)
        denominators = jnp.transpose(lax.optimization_barrier(jnp.sum(cross_weight, axis=(2, 3))))
        return (numerators / denominators[:, :, None]).reshape(ANS, hd_total).astype(jnp.bfloat16)
    return lax.map(one_question, jnp.arange(Q).astype(jnp.int32))
```

```python
import functools

import jax
import jax.numpy as jnp
from jax import lax
from jax.experimental import pallas as pl
from jax.experimental.pallas import tpu as pltpu
from jax.sharding import PartitionSpec as P

MESH = pl.DeviceIdType.MESH
BF16, F32 = jnp.bfloat16, jnp.float32
ZN, XN, YN = 8, 4, 8
CAP = 3
HEAD_DIM = 64
NORM_EPSILON = 1e-06
FAR_FIRST = (4, 3, 5, 2, 6, 1, 7)
NT = (((1,), (1,)), ((), ()))


def wrap(value, size):
    return lax.rem(value + size, size)


def dot_nt(a, b):
    return lax.dot_general(a, b, NT, preferred_element_type=F32)


def kernel(
    meta, qs, cache, gain, wq, wk, wv, wo, dwk_hbm, dwv_hbm, dq,
    out,
    wg, wot, wot_own, xg, qg, dqg, xn, ctxg, enc, ekeys, dqp, cs, cr, cwg, ns, nr, t1s, t1r, t2s, t2r, dwk, dwv,
    load_sem, ring_send, ring1, ring2, sib_recv, yx_send, yx_recv,
    qz_s, qz_r, qx_s, qx_r, qs_s, qs_r, qy_s, qy_r,
    wp_s, wp_r, wz_s, wz_r, wx_s, wx_r, ws_s, ws_r,
    cx_s, cx_r, a_s, a_r, b_s, b_r, n_s, n_r, f_s, f_r, h_s, h_r,
):
    m = lax.axis_index("mem")
    y = lax.axis_index("dec")
    z = m // (2 * XN)
    x = lax.rem(m // 2, XN)
    core = lax.rem(m, 2)
    r8 = lax.rem(m, 8)

    def device(zz, xx, cc, yy):
        return ((zz * XN + xx) * 2 + cc, yy)

    def at_z(k):
        return device(wrap(z + k, ZN), x, core, y)

    def at_x(k):
        return device(z, wrap(x + k, XN), core, y)

    def at_y(k):
        return device(z, x, core, wrap(y + k, YN))

    def at_xc(k):
        other = lax.rem(r8 + k, 8)
        return (z * 8 + other, y)

    sibling = device(z, x, 1 - core, y)
    swap = (8 * y + r8, z)
    has_swap = z != y

    def remote(src, dst, send, recv, to):
        return pltpu.make_async_remote_copy(
            src_ref=src, dst_ref=dst, send_sem=send, recv_sem=recv, device_id=to, device_id_type=MESH
        )

    barrier = pltpu.get_barrier_semaphore()
    for k in range(1, 8):
        pl.semaphore_signal(barrier, inc=1, device_id=at_y(k), device_id_type=MESH)
        pl.semaphore_signal(barrier, inc=1, device_id=at_z(k), device_id_type=MESH)
        pl.semaphore_signal(barrier, inc=1, device_id=at_xc(k), device_id_type=MESH)

    @pl.when(has_swap)
    def _():
        pl.semaphore_signal(barrier, inc=1, device_id=swap, device_id_type=MESH)

    load_k = pltpu.make_async_copy(dwk_hbm, dwk, load_sem.at[0])
    load_v = pltpu.make_async_copy(dwv_hbm, dwv, load_sem.at[1])
    load_k.start()
    load_v.start()

    first = qs[0].astype(F32)
    second = jnp.concatenate([first[:, 384:512], dq[0].astype(F32)], axis=1)
    own_q = (core * XN + x) * ZN + z
    qg[own_q] = jnp.concatenate([first[:, 0:384], second], axis=0).astype(BF16)
    wg[m] = jnp.concatenate([wq[...], wk[...], wv[...]], axis=1)
    turned = jnp.transpose(wo[...].astype(F32)).astype(BF16)
    wot_own[...] = turned
    own_w = (core * XN + x) * ZN + z

    @pl.when(jnp.logical_not(has_swap))
    def _():
        wot[own_w] = wot_own[...]

    for c in range(CAP):
        xg[y, 64 * c : 64 * c + 64, :] = cache[meta[c]]

    @pl.when(has_swap)
    def _():
        pl.semaphore_wait(barrier, 22)

    @pl.when(jnp.logical_not(has_swap))
    def _():
        pl.semaphore_wait(barrier, 21)

    def q_z(k, source):
        sl = qg.at[(core * XN + x) * ZN + wrap(source, ZN)]
        return remote(sl, sl, qz_s.at[k], qz_r.at[k], at_z(k))

    def q_x(k, source):
        sl = qg.at[pl.ds((core * XN + wrap(source, XN)) * ZN, ZN)]
        return remote(sl, sl, qx_s.at[k], qx_r.at[k], at_x(k))

    def q_s(cc):
        sl = qg.at[pl.ds(cc * (XN * ZN), XN * ZN)]
        return remote(sl, sl, qs_s.at[0], qs_r.at[0], sibling)

    def q_y(k, source):
        sl = xg.at[wrap(source, YN), pl.ds(192, 32)]
        sd = dqg.at[wrap(source, YN)]
        return (
            remote(sl, sl, qy_s.at[0, k], qy_r.at[0, k], at_y(k)),
            remote(sd, sd, qy_s.at[1, k], qy_r.at[1, k], at_y(k)),
        )

    def question_0():
        for k in FAR_FIRST:
            q_z(k, z).start()

    def question_1():
        for k in FAR_FIRST:
            q_z(k, z - k).wait_recv()
        for k in (2, 1, 3):
            q_x(k, x).start()

    def question_2():
        for k in (1, 2, 3):
            q_x(k, x - k).wait_recv()
        q_s(core).start()

    def question_3():
        q_s(1 - core).wait_recv()
        rows, queries = [], []
        for c in range(CAP):
            asked = qg[meta[4 + c]].astype(F32)
            rows.append(jnp.concatenate([asked[0:8], asked[8:16, 0:128]], axis=1))
            queries.append(asked[8:16, 128:384])
        rows.append(jnp.zeros((8, 512), F32))
        queries.append(jnp.zeros((8, 256), F32))
        xg[y, 192:224, :] = jnp.concatenate(rows, axis=0).astype(BF16)
        dqg[y] = jnp.concatenate(queries, axis=0).astype(BF16)
        for k in FAR_FIRST:
            for copy in q_y(k, y):
                copy.start()

    def question_end():
        for k in FAR_FIRST:
            for copy in q_y(k, y - k):
                copy.wait_recv()

    def w_swap():
        return remote(wot_own, wot.at[(lax.rem(r8, 2) * XN + r8 // 2) * ZN + y], wp_s.at[0], wp_r.at[0], swap)

    def w_z(k, source):
        sl = wot.at[(core * XN + x) * ZN + wrap(source, ZN)]
        return remote(sl, sl, wz_s.at[k], wz_r.at[k], at_z(k))

    def w_x(k, source):
        sl = wot.at[pl.ds((core * XN + wrap(source, XN)) * ZN, ZN)]
        return remote(sl, sl, wx_s.at[k], wx_r.at[k], at_x(k))

    def w_s(cc):
        sl = wot.at[pl.ds(cc * (XN * ZN), XN * ZN)]
        return remote(sl, sl, ws_s.at[0], ws_r.at[0], sibling)

    def wout_0():
        @pl.when(has_swap)
        def _():
            w_swap().start()

    def wout_1():
        @pl.when(has_swap)
        def _():
            w_swap().wait_recv()

        for k in FAR_FIRST:
            w_z(k, z).start()

    def wout_2():
        for k in FAR_FIRST:
            w_z(k, z - k).wait_recv()
        for k in (2, 1, 3):
            w_x(k, x).start()

    def wout_3():
        for k in (1, 2, 3):
            w_x(k, x - k).wait_recv()
        w_s(core).start()

    def y_copy(c, sign, step, source):
        if step < YN // 2:
            sl = xg.at[wrap(source, YN), pl.ds(64 * c, 64)]
        else:
            sl = xg.at[wrap(source, YN), pl.ds(64 * c + (0 if sign > 0 else 32), 32)]
        d = 0 if sign > 0 else 1
        return remote(sl, sl, yx_send.at[c, d, step], yx_recv.at[c, d, step], at_y(sign))

    def rows_step(step):
        for c in range(CAP):
            for sign in (1, -1):
                if step > 0:
                    y_copy(c, sign, step, y - sign * step).wait_recv()
                if step < YN // 2:
                    y_copy(c, sign, step + 1, y - sign * step).start()

    def weights(role):
        n1, n2 = (ZN, XN) if role == 0 else (XN, ZN)
        i1, i2 = (z, x) if role == 0 else (x, z)
        sends = []

        def near(dim, sign):
            along_z = (dim == 1) == (role == 0)
            return at_z(sign) if along_z else at_x(sign)

        def chip(o, p):
            a, b = wrap(i1 + o, n1), wrap(i2 + p, n2)
            return a * XN + b if role == 0 else b * XN + a

        def view(o, p, half):
            index = chip(o, p) * 2 + role
            return wg.at[index] if half is None else wg.at[index, pl.ds(32 * half, 32)]

        def copy(o, p, half, recv, to, number):
            sl = view(o, p, half)
            return remote(sl, sl, ring_send.at[number], recv, to)

        def start(o, p, half, recv, to):
            copy(o, p, half, recv, to, len(sends)).start()
            sends.append(half)

        def hand_over(o, p):
            start(o, p, None, sib_recv.at[chip(o, p)], sibling)

        def half_of(sign):
            return 0 if sign > 0 else 1

        def pass_on(dim, o, p, sign, step):
            count = n1 if dim == 1 else n2
            half = half_of(sign) if step == count // 2 else None
            recv = ring1.at[half_of(sign), step] if dim == 1 else ring2.at[o % n1, half_of(sign), step]
            start(o, p, half, recv, near(dim, sign))

        def arrived(dim, o, p, sign, step):
            count = n1 if dim == 1 else n2
            half = half_of(sign) if step == count // 2 else None
            recv = ring1.at[half_of(sign), step] if dim == 1 else ring2.at[o % n1, half_of(sign), step]
            copy(o, p, half, recv, near(dim, sign), 0).wait_recv()

        def second(o):
            for sign in (1, -1):
                pass_on(2, o, 0, sign, 1)
            hand_over(o, 0)

        def arrive_1(step):
            for sign in (1, -1):
                arrived(1, -sign * step, 0, sign, step)
                if step < n1 // 2:
                    pass_on(1, -sign * step, 0, sign, step + 1)
                    second(-sign * step)
            if step == n1 // 2:
                second(step)

        def arrive_2(o, step):
            for sign in (1, -1):
                arrived(2, o, -sign * step, sign, step)
                if step < n2 // 2:
                    pass_on(2, o, -sign * step, sign, step + 1)
                    hand_over(o, -sign * step)
            if step == n2 // 2:
                hand_over(o, step)

        for time in range(n1 // 2 + n2 // 2 + 1):
            if time == 0:
                question_0()
                wout_0()
                for sign in (1, -1):
                    pass_on(1, 0, 0, sign, 1)
                second(0)
            elif time <= n1 // 2:
                arrive_1(time)
            if time <= YN // 2:
                rows_step(time)
            for step in range(1, n2 // 2 + 1):
                o = time - step
                if 0 <= o <= n1 // 2:
                    for signed in (o,) if o in (0, n1 // 2) else (o, -o):
                        arrive_2(signed, step)
            if time == 1:
                question_1()
            if time == 2:
                question_2()
            if time == 3:
                question_3()
            if time == 4:
                wout_1()
        return sends

    sends = [None, None]
    for role in (0, 1):

        @pl.when(core == role)
        def _():
            sends[role] = weights(role)

    for chip in range(ZN * XN):
        sl = wg.at[chip * 2 + (1 - core)]
        remote(sl, sl, ring_send.at[0], sib_recv.at[chip], sibling).wait_recv()
    question_end()
    wout_2()

    squares = jnp.zeros((224, 128), F32)
    for d in range(YN):
        block = xg[d].astype(F32)
        block = block * block
        squares += block[:, 0:128] + block[:, 128:256] + block[:, 256:384] + block[:, 384:512]
    inverse = lax.rsqrt(jnp.sum(squares, axis=1, keepdims=True) * (1.0 / (512 * YN)) + NORM_EPSILON)
    for d in range(YN):
        xn[:, 512 * d : 512 * d + 512] = (xg[d].astype(F32) * inverse * gain[d : d + 1, :]).astype(BF16)
    totals = []
    for part in range(3):
        weight = wg[:, :, 256 * part : 256 * part + 256].reshape(4096, 256)
        totals.append(jnp.dot(xn[...], weight, preferred_element_type=F32).astype(BF16))
    queries, keys, values = totals

    def pair_of(index):
        return jnp.where(index < 192, index // 64, jnp.minimum((index - 192) // 8, CAP - 1))

    row_ids = lax.broadcasted_iota(jnp.int32, (224, 224), 0)
    col_ids = lax.broadcasted_iota(jnp.int32, (224, 224), 1)
    col_pair = pair_of(col_ids)
    length = jnp.where(col_pair == 0, meta[8], jnp.where(col_pair == 1, meta[9], meta[10]))
    token = col_ids - 192 - 8 * col_pair
    live = (pair_of(row_ids) == col_pair) & (token < length)

    def ctx_copy(part, k, source, half):
        if half is None:
            sl = ctxg.at[wrap(source, YN), part]
        else:
            sl = ctxg.at[wrap(source, YN), part, pl.ds(112 * half, 112)]
        return sl

    def ctx_near(part, k):
        sl = ctx_copy(part, k, y, None)
        return remote(sl, sl, cx_s.at[part, k], cx_r.at[part, k], at_y(k - 3))

    for part in range(2):
        outs = []
        for h in (2 * part, 2 * part + 1):
            sl = slice(64 * h, 64 * h + 64)
            scores = dot_nt(queries[:, sl], keys[:, sl]) * (HEAD_DIM**-0.5)
            weight = jnp.where(live, jnp.exp(scores), 0.0)
            prob = (weight / jnp.sum(weight, axis=1, keepdims=True)).astype(BF16)
            outs.append(jnp.dot(prob, values[:, sl], preferred_element_type=F32))
        ctxg[y, part] = jnp.concatenate(outs, axis=1).astype(BF16)
        for k in (-2, 2, -1, 1):
            ctx_near(part, k + 3).start()

    def ctx_recv(part, k, half=None):
        sl = ctx_copy(part, k, y - k, half)
        return sl

    def ctx_wait(part, k, half=None):
        sl = ctx_recv(part, k, half)
        slot = k + 3 if abs(k) <= 2 else {3: 6, -3: 7, 4: 8, -4: 9}[k]
        remote(sl, sl, cx_s.at[part, 0], cx_r.at[part, slot], at_y(1)).wait_recv()

    def ctx_forward(part, sign):
        sl = ctx_copy(part, 0, y - 2 * sign, None)
        slot = 6 if sign > 0 else 7
        remote(sl, sl, cx_s.at[part, slot], cx_r.at[part, slot], at_y(sign)).start()
        half = 0 if sign > 0 else 1
        sl = ctx_copy(part, 0, y - 2 * sign, half)
        slot = 8 if sign > 0 else 9
        remote(sl, sl, cx_s.at[part, slot], cx_r.at[part, slot], at_y(2 * sign)).start()

    load_k.wait()
    lane_head = lax.broadcasted_iota(jnp.int32, (8, 256), 1) // 64
    for g in range(YN):
        asked = dqg[g].astype(F32)
        blocks = []
        for c in range(CAP):
            for h in range(4):
                blocks.append(jnp.where(lane_head == h, asked[8 * c : 8 * c + 8], 0.0))
        spread = jnp.concatenate(blocks, axis=0).astype(BF16)
        product = dot_nt(spread, dwk[:, 256 * g : 256 * g + 256]).astype(BF16)
        for c in range(CAP):
            dqp[c, 32 * g : 32 * g + 32, :] = product[32 * c : 32 * c + 32]

    for part in range(2):
        for sign in (1, -1):
            ctx_wait(part, 2 * sign)
            ctx_forward(part, sign)
    wout_3()
    for part in range(2):
        for sign in (1, -1):
            ctx_wait(part, sign)
            ctx_wait(part, 3 * sign)
            ctx_wait(part, 4 * sign, 0 if sign > 0 else 1)
    w_s(1 - core).wait_recv()

    attended = jnp.zeros((224, 512), F32)
    for d in range(YN):
        context = jnp.concatenate([ctxg[d, 0], ctxg[d, 1]], axis=1)
        weight = jnp.concatenate(
            [wot[((r % 2) * XN + r // 2) * ZN + d] for r in range(8)], axis=0
        )
        attended += dot_nt(context, weight)
    enc[...] = (xg[y].astype(F32) + attended).astype(BF16)

    for c in range(CAP):
        ekeys[c, 0:64, :] = enc[64 * c : 64 * c + 64, :]
        ekeys[c, 64:96, :] = enc[192:224, :]
        ekeys[c, 96:128, :] = jnp.zeros((32, 512), BF16)
        part = dot_nt(dqp[c], ekeys[c]).astype(BF16)
        for g in range(YN):
            cs[g, 32 * c : 32 * c + 32, :] = part[32 * g : 32 * g + 32]

    def scatter(src, dst, send, recv, k):
        return remote(src.at[wrap(y + k, YN)], dst.at[y], send.at[k], recv.at[k], at_y(k))

    def scattered(src, dst, send, recv, k):
        sl = dst.at[wrap(y - k, YN)]
        return remote(sl, sl, send.at[k], recv.at[k], at_y(k))

    for k in FAR_FIRST:
        scatter(cs, cr, a_s, a_r, k).start()
    for k in FAR_FIRST:
        scattered(cs, cr, a_s, a_r, k).wait_recv()
    total = cs[y].astype(F32)
    for k in range(1, 8):
        total += cr[wrap(y - k, YN)].astype(F32)
    lanes = lax.broadcasted_iota(jnp.int32, (32, 128), 1)
    masks = []
    for c in range(CAP):
        spot = lanes - 64 - 8 * c
        masks.append((lanes < 64) | ((spot >= 0) & (spot < meta[8 + c])))
    cross = jnp.concatenate(
        [jnp.where(masks[c], jnp.exp(total[32 * c : 32 * c + 32] * (HEAD_DIM**-0.5)), 0.0) for c in range(CAP)], axis=0
    )
    den = jnp.sum(cross, axis=1, keepdims=True)
    cwg[y] = cross.astype(BF16)
    sl = cwg.at[y]
    for k in FAR_FIRST:
        remote(sl, sl, b_s.at[k], b_r.at[k], at_y(k)).start()
    load_v.wait()
    for k in FAR_FIRST:
        scattered(cwg, cwg, b_s, b_r, k).wait_recv()

    mixed = []
    for c in range(CAP):
        cw = jnp.concatenate([cwg[g, 32 * c : 32 * c + 32] for g in range(YN)], axis=0)
        mixed.append(jnp.dot(cw, ekeys[c], preferred_element_type=F32).astype(BF16))
    for g in range(YN):
        left = jnp.concatenate([mixed[c][32 * g : 32 * g + 32] for c in range(CAP)], axis=0)
        product = jnp.dot(left, dwv[:, 256 * g : 256 * g + 256], preferred_element_type=F32)
        rows = []
        for c in range(CAP):
            row = jnp.zeros((8, 256), F32)
            for h in range(4):
                low = 32 * c + 8 * h
                row += jnp.where(lane_head == h, product[low : low + 8], 0.0)
            rows.append(row)
        rows.append(jnp.zeros((8, 256), F32))
        ns[g] = jnp.concatenate(rows, axis=0).astype(BF16)
    for k in FAR_FIRST:
        scatter(ns, nr, n_s, n_r, k).start()
    for k in FAR_FIRST:
        scattered(ns, nr, n_s, n_r, k).wait_recv()
    num = ns[y].astype(F32)
    for k in range(1, 8):
        num += nr[wrap(y - k, YN)].astype(F32)

    packed = []
    for c in range(CAP):
        wide = jnp.zeros((8, 256), F32)
        for h in range(4):
            low = 32 * c + 8 * h
            wide = jnp.where(lane_head == h, den[low : low + 8], wide)
        packed.append(jnp.concatenate([num[8 * c : 8 * c + 8], wide], axis=0))
    for spot in range(8):
        for zz in range(ZN):
            question = zz * 8 + spot
            value = jnp.zeros((16, 256), F32)
            for c in range(CAP):
                value += jnp.where(meta[12 + c] == question, packed[c], 0.0)
            t1s[spot, zz] = value.astype(BF16)
    for k in FAR_FIRST:
        remote(t1s.at[lax.rem(r8 + k, 8)], t1r.at[r8], f_s.at[k], f_r.at[k], at_xc(k)).start()
    for k in FAR_FIRST:
        sl = t1r.at[lax.rem(r8 + 8 - k, 8)]
        remote(sl, sl, f_s.at[k], f_r.at[k], at_xc(k)).wait_recv()
    gathered = t1s[r8].astype(F32)
    for k in range(1, 8):
        gathered += t1r[lax.rem(r8 + 8 - k, 8)].astype(F32)
    t2s[...] = gathered.astype(BF16)
    for k in FAR_FIRST:
        remote(t2s.at[wrap(z + k, ZN)], t2r.at[z], h_s.at[k], h_r.at[k], at_z(k)).start()
    for k in FAR_FIRST:
        sl = t2r.at[wrap(z - k, ZN)]
        remote(sl, sl, h_s.at[k], h_r.at[k], at_z(k)).wait_recv()
    answer = t2s[z].astype(F32)
    for k in range(1, 8):
        answer += t2r[wrap(z - k, ZN)].astype(F32)
    out[0] = (answer[0:8] / answer[8:16]).astype(BF16)

    for role in (0, 1):

        @pl.when(core == role)
        def _():
            for number, half in enumerate(sends[role]):
                sl = wg.at[0] if half is None else wg.at[0, pl.ds(0, 32)]
                remote(sl, sl, ring_send.at[number], sib_recv.at[0], sibling).wait_send()

    @pl.when(has_swap)
    def _():
        w_swap().wait_send()

    q_s(core).wait_send()
    w_s(core).wait_send()
    for k in (1, 2, 3):
        q_x(k, x).wait_send()
        w_x(k, x).wait_send()
    for c in range(CAP):
        for sign in (1, -1):
            for step in range(1, YN // 2 + 1):
                y_copy(c, sign, step, y).wait_send()
    for part in range(2):
        for slot in (1, 2, 4, 5, 6, 7, 8, 9):
            sl = ctx_copy(part, 0, y, None if slot < 8 else 0)
            remote(sl, sl, cx_s.at[part, slot], cx_r.at[part, slot], at_y(1)).wait_send()
    for k in range(1, 8):
        q_z(k, z).wait_send()
        w_z(k, z).wait_send()
        for copy in q_y(k, y):
            copy.wait_send()
        scatter(cs, cr, a_s, a_r, k).wait_send()
        scatter(cwg, cwg, b_s, b_r, k).wait_send()
        scatter(ns, nr, n_s, n_r, k).wait_send()
        remote(t1s.at[0], t1r.at[0], f_s.at[k], f_r.at[k], at_xc(k)).wait_send()
        remote(t2s.at[0], t2r.at[0], h_s.at[k], h_r.at[k], at_z(k)).wait_send()


def routing(passage_ids, location, question_lengths, mem_index):
    request_total = passage_ids.size
    pass_count = passage_ids.shape[1]
    row = jnp.take(location, passage_ids.reshape(-1))
    served = row // 4 == mem_index
    order = jnp.arange(request_total)
    rank = jnp.sum((served[None, :] & (order[None, :] < order[:, None])).astype(jnp.int32), axis=1)
    taken = served[None, :] & (rank[None, :] == jnp.arange(4)[:, None])
    question = order // pass_count
    lengths = jnp.broadcast_to(question_lengths[:, None], passage_ids.shape).reshape(-1)
    spot = ((question % 2) * XN + (question // 2) % XN) * ZN + question // (2 * XN)

    def pick(values, empty):
        return jnp.sum(jnp.where(taken, values[None, :] - empty, 0), axis=1) + empty

    return jnp.concatenate(
        [pick(row % 4, 0), pick(spot, 0), pick(lengths, 0), pick(question, -1)]
    ).astype(jnp.int32)


def body(
    question_states, passage_cache, norm_gain, enc_wq, enc_wk, enc_wv, enc_wo, dec_wk, dec_wv, dec_queries,
    passage_ids, location, question_lengths,
):
    meta = routing(passage_ids, location, question_lengths, lax.axis_index("mem"))
    vmem = pl.BlockSpec(memory_space=pltpu.VMEM)
    anywhere = pl.BlockSpec(memory_space=pl.ANY)
    dma = pltpu.SemaphoreType.DMA
    return pl.pallas_call(
        kernel,
        name="step",
        out_shape=jax.ShapeDtypeStruct((1, 8, 256), BF16),
        in_specs=[pl.BlockSpec(memory_space=pltpu.SMEM)] + [vmem] * 7 + [anywhere] * 2 + [vmem],
        out_specs=vmem,
        scratch_shapes=[
            pltpu.VMEM((64, 64, 768), BF16),
            pltpu.VMEM((64, 64, 256), BF16),
            pltpu.VMEM((64, 256), BF16),
            pltpu.VMEM((8, 224, 512), BF16),
            pltpu.VMEM((64, 16, 384), BF16),
            pltpu.VMEM((8, 32, 256), BF16),
            pltpu.VMEM((224, 4096), BF16),
            pltpu.VMEM((8, 2, 224, 128), BF16),
            pltpu.VMEM((224, 512), BF16),
            pltpu.VMEM((3, 128, 512), BF16),
            pltpu.VMEM((3, 256, 512), BF16),
            pltpu.VMEM((8, 96, 128), BF16),
            pltpu.VMEM((8, 96, 128), BF16),
            pltpu.VMEM((8, 96, 128), BF16),
            pltpu.VMEM((8, 32, 256), BF16),
            pltpu.VMEM((8, 32, 256), BF16),
            pltpu.VMEM((8, 8, 16, 256), BF16),
            pltpu.VMEM((8, 8, 16, 256), BF16),
            pltpu.VMEM((8, 16, 256), BF16),
            pltpu.VMEM((8, 16, 256), BF16),
            pltpu.VMEM((512, 2048), BF16),
            pltpu.VMEM((512, 2048), BF16),
            dma((2,)),
            dma((80,)),
            dma((2, 5)),
            dma((8, 2, 5)),
            dma((32,)),
            dma((3, 2, 5)),
            dma((3, 2, 5)),
            dma((8,)), dma((8,)), dma((4,)), dma((4,)), dma((1,)), dma((1,)), dma((2, 8)), dma((2, 8)),
            dma((1,)), dma((1,)), dma((8,)), dma((8,)), dma((4,)), dma((4,)), dma((1,)), dma((1,)),
            dma((2, 10)), dma((2, 10)),
            dma((8,)), dma((8,)), dma((8,)), dma((8,)), dma((8,)), dma((8,)), dma((8,)), dma((8,)), dma((8,)), dma((8,)),
        ],
        compiler_params=pltpu.CompilerParams(
            collective_id=0, has_side_effects=True, vmem_limit_bytes=56 * 2**20
        ),
    )(
        meta, question_states, passage_cache, norm_gain.reshape(8, 512), enc_wq, enc_wk, enc_wv, enc_wo,
        dec_wk, dec_wv, dec_queries,
    )


def solution(mesh):
    in_specs = (
        P("mem", None, "dec"),
        P("mem", None, "dec"),
        P(),
        P("mem", "dec"),
        P("mem", "dec"),
        P("mem", "dec"),
        P("dec", "mem"),
        P("dec", None),
        P("dec", None),
        P("mem", None, "dec"),
        P(),
        P(),
        P(),
    )
    return jax.shard_map(body, mesh=mesh, in_specs=in_specs, out_specs=P("mem", None, "dec"), check_vma=False)
```

```python
import functools

import jax
import jax.numpy as jnp
from jax import lax
from jax.experimental import pallas as pl
from jax.experimental.pallas import tpu as pltpu
from jax.sharding import PartitionSpec as P

MESH = pl.DeviceIdType.MESH
BF16, F32 = jnp.bfloat16, jnp.float32
ZN, XN, YN = 8, 4, 8
CAP = 3
SUBS = 1
DIRECT = ((False, False), (False, False))
HEAD_DIM = 64
NORM_EPSILON = 1e-06
FAR_FIRST = (4, 3, 5, 2, 6, 1, 7)
NT = (((1,), (1,)), ((), ()))


def wrap(value, size):
    return lax.rem(value + size, size)


def dot_nt(a, b):
    return lax.dot_general(a, b, NT, preferred_element_type=F32)


def kernel(
    ids, rows_of, lengths, qs, cache, gain, wq, wk, wv, wo, dwk_hbm, dwv_hbm, dq,
    out,
    wg, wot, wot_own, xg, qg, dqg, xn, ctxg, enc, ekeys, dqp, cs, cr, cwg, ns, nr, t1s, t1r, t2s, t2r, dwk, dwv,
    load_sem, ring_send, ring1, ring2, sib_recv, yx_send, yx_recv,
    qz_s, qz_r, qx_s, qx_r, qs_s, qs_r, qy_s, qy_r,
    wp_s, wp_r, wz_s, wz_r, wx_s, wx_r, ws_s, ws_r,
    cx_s, cx_r, a_s, a_r, b_s, b_r, n_s, n_r, f_s, f_r, h_s, h_r,
):
    m = lax.axis_index("mem")
    y = lax.axis_index("dec")
    z = m // (2 * XN)
    x = lax.rem(m // 2, XN)
    core = lax.rem(m, 2)
    r8 = lax.rem(m, 8)

    def device(zz, xx, cc, yy):
        return ((zz * XN + xx) * 2 + cc, yy)

    def at_z(k):
        return device(wrap(z + k, ZN), x, core, y)

    def at_x(k):
        return device(z, wrap(x + k, XN), core, y)

    def at_y(k):
        return device(z, x, core, wrap(y + k, YN))

    def at_xc(k):
        other = lax.rem(r8 + k, 8)
        return (z * 8 + other, y)

    sibling = device(z, x, 1 - core, y)
    swap = (8 * y + r8, z)
    has_swap = z != y

    def remote(src, dst, send, recv, to):
        return pltpu.make_async_remote_copy(
            src_ref=src, dst_ref=dst, send_sem=send, recv_sem=recv, device_id=to, device_id_type=MESH
        )

    barrier = pltpu.get_barrier_semaphore()
    for k in range(1, 8):
        pl.semaphore_signal(barrier, inc=1, device_id=at_y(k), device_id_type=MESH)
        pl.semaphore_signal(barrier, inc=1, device_id=at_z(k), device_id_type=MESH)
        pl.semaphore_signal(barrier, inc=1, device_id=at_xc(k), device_id_type=MESH)

    @pl.when(has_swap)
    def _():
        pl.semaphore_signal(barrier, inc=1, device_id=swap, device_id_type=MESH)

    load_k = pltpu.make_async_copy(dwk_hbm, dwk, load_sem.at[0])
    load_v = pltpu.make_async_copy(dwv_hbm, dwv, load_sem.at[1])
    load_k.start()
    load_v.start()

    first = qs[0].astype(F32)
    second = jnp.concatenate([first[:, 384:512], dq[0].astype(F32)], axis=1)
    own_q = (core * XN + x) * ZN + z
    qg[own_q] = jnp.concatenate([first[:, 0:384], second], axis=0).astype(BF16)
    wg[m] = jnp.concatenate([wq[...], wk[...], wv[...]], axis=1)
    wot_own[...] = wo[...]
    own_w = (core * XN + x) * ZN + z

    @pl.when(jnp.logical_not(has_swap))
    def _():
        wot[own_w] = wot_own[...]

    def look(index, found):
        count, slots, asking = found
        question, pick = index // 2, lax.rem(index, 2)
        place = rows_of[ids[pick, question]] - 4 * m
        hit = (place >= 0) & (place < 4)
        taken = [hit & (count == c) for c in range(CAP)]
        return (
            count + jnp.where(hit, 1, 0),
            tuple(jnp.where(taken[c], place, slots[c]) for c in range(CAP)),
            tuple(jnp.where(taken[c], question, asking[c]) for c in range(CAP)),
        )

    zero, none = jnp.int32(0), jnp.int32(-1)
    _, slots, asking = lax.fori_loop(0, 2 * 64, look, (zero, (zero,) * CAP, (none,) * CAP), unroll=8)
    asked_question = [jnp.maximum(asking[c], 0) for c in range(CAP)]
    length_of = [lengths[asked_question[c]] for c in range(CAP)]
    for c in range(CAP):
        xg[y, 64 * c : 64 * c + 64, :] = cache[slots[c]]

    @pl.when(has_swap)
    def _():
        pl.semaphore_wait(barrier, 22)

    @pl.when(jnp.logical_not(has_swap))
    def _():
        pl.semaphore_wait(barrier, 21)

    def q_z(k, source):
        sl = qg.at[(core * XN + x) * ZN + wrap(source, ZN)]
        return remote(sl, sl, qz_s.at[k], qz_r.at[k], at_z(k))

    def q_x(k, source):
        sl = qg.at[pl.ds((core * XN + wrap(source, XN)) * ZN, ZN)]
        return remote(sl, sl, qx_s.at[k], qx_r.at[k], at_x(k))

    def q_s(cc):
        sl = qg.at[pl.ds(cc * (XN * ZN), XN * ZN)]
        return remote(sl, sl, qs_s.at[0], qs_r.at[0], sibling)

    def q_y(which, k, source):
        sl = (dqg.at[wrap(source, YN)], xg.at[wrap(source, YN), pl.ds(192, 32)])[which]
        return remote(sl, sl, qy_s.at[which, k], qy_r.at[which, k], at_y(k))

    def question_0():
        for k in FAR_FIRST:
            q_z(k, z).start()

    def question_1():
        for k in FAR_FIRST:
            q_z(k, z - k).wait_recv()
        for k in (2, 1, 3):
            q_x(k, x).start()

    def question_2():
        for k in (1, 2, 3):
            q_x(k, x - k).wait_recv()
        q_s(core).start()

    def question_3():
        q_s(1 - core).wait_recv()
        rows, queries = [], []
        for c in range(CAP):
            q = asked_question[c]
            asked = qg[(lax.rem(q, 2) * XN + lax.rem(q // 2, XN)) * ZN + q // (2 * XN)].astype(F32)
            rows.append(jnp.concatenate([asked[0:8], asked[8:16, 0:128]], axis=1))
            queries.append(asked[8:16, 128:384])
        rows.append(jnp.zeros((8, 512), F32))
        queries.append(jnp.zeros((8, 256), F32))
        xg[y, 192:224, :] = jnp.concatenate(rows, axis=0).astype(BF16)
        dqg[y] = jnp.concatenate(queries, axis=0).astype(BF16)
        for which in (1, 0):
            for k in FAR_FIRST:
                q_y(which, k, y).start()

    def question_end(which):
        for k in FAR_FIRST:
            q_y(which, k, y - k).wait_recv()

    def w_swap():
        return remote(wot_own, wot.at[(lax.rem(r8, 2) * XN + r8 // 2) * ZN + y], wp_s.at[0], wp_r.at[0], swap)

    def w_z(k, source):
        sl = wot.at[(core * XN + x) * ZN + wrap(source, ZN)]
        return remote(sl, sl, wz_s.at[k], wz_r.at[k], at_z(k))

    def w_x(k, source):
        sl = wot.at[pl.ds((core * XN + wrap(source, XN)) * ZN, ZN)]
        return remote(sl, sl, wx_s.at[k], wx_r.at[k], at_x(k))

    def w_s(cc):
        sl = wot.at[pl.ds(cc * (XN * ZN), XN * ZN)]
        return remote(sl, sl, ws_s.at[0], ws_r.at[0], sibling)

    def wout_0():
        @pl.when(has_swap)
        def _():
            w_swap().start()

    def wout_1():
        @pl.when(has_swap)
        def _():
            w_swap().wait_recv()

        for k in FAR_FIRST:
            w_z(k, z).start()

    def wout_2():
        for k in FAR_FIRST:
            w_z(k, z - k).wait_recv()
        for k in (2, 1, 3):
            w_x(k, x).start()

    def wout_3():
        for k in (1, 2, 3):
            w_x(k, x - k).wait_recv()
        w_s(core).start()

    def y_copy(c, sign, step, source):
        if step < YN // 2:
            sl = xg.at[wrap(source, YN), pl.ds(64 * c, 64)]
        else:
            sl = xg.at[wrap(source, YN), pl.ds(64 * c + (0 if sign > 0 else 32), 32)]
        d = 0 if sign > 0 else 1
        return remote(sl, sl, yx_send.at[c, d, step], yx_recv.at[c, d, step], at_y(sign))

    def rows_step(step):
        for c in range(CAP):
            for sign in (1, -1):
                if step > 0:
                    y_copy(c, sign, step, y - sign * step).wait_recv()
                if step < YN // 2:
                    y_copy(c, sign, step + 1, y - sign * step).start()

    def weights(role):
        n1, n2 = (ZN, XN) if role == 0 else (XN, ZN)
        i1, i2 = (z, x) if role == 0 else (x, z)
        direct_1, direct_2 = DIRECT[role]
        sends = []

        def away(dim, distance):
            along_z = (dim == 1) == (role == 0)
            return at_z(distance) if along_z else at_x(distance)

        def chip(o, p):
            a, b = wrap(i1 + o, n1), wrap(i2 + p, n2)
            return a * XN + b if role == 0 else b * XN + a

        def copy(o, p, sub, half, recv, to, number):
            rows = 64 // SUBS
            low = sub * rows
            if half is not None:
                rows = rows // 2
                low += half * rows
            sl = wg.at[chip(o, p) * 2 + role, pl.ds(low, rows)]
            return remote(sl, sl, ring_send.at[number], recv, to)

        def start(o, p, sub, half, recv, to):
            copy(o, p, sub, half, recv, to, len(sends)).start()
            sends.append(half)

        def hand_over(o, p, sub):
            start(o, p, sub, None, sib_recv.at[chip(o, p), sub], sibling)

        def way(sign):
            return 0 if sign > 0 else 1

        def receipt(dim, o, sign, step, sub):
            return ring1.at[way(sign), step, sub] if dim == 1 else ring2.at[o % n1, way(sign), step, sub]

        def half_at(dim, sign, step):
            count, direct = (n1, direct_1) if dim == 1 else (n2, direct_2)
            return way(sign) if step == count // 2 and not direct else None

        def spread(dim, o, sub):
            count, direct = (n1, direct_1) if dim == 1 else (n2, direct_2)
            if not direct:
                for sign in (1, -1):
                    start(o, 0, sub, half_at(dim, sign, 1), receipt(dim, o, sign, 1, sub), away(dim, sign))
                return
            for step in range(count // 2, 0, -1):
                for sign in (1, -1) if step < count // 2 else (1,):
                    start(o, 0, sub, None, receipt(dim, o, sign, step, sub), away(dim, sign * step))

        def arrive(dim, o, sign, step, sub):
            count, direct = (n1, direct_1) if dim == 1 else (n2, direct_2)
            last = step == count // 2
            if direct and last and sign < 0:
                return False
            place = (-sign * step, 0) if dim == 1 else (o, -sign * step)
            half = half_at(dim, sign, step)
            copy(*place, sub, half, receipt(dim, o, sign, step, sub), away(dim, sign), 0).wait_recv()
            if not direct and not last:
                onward = half_at(dim, sign, step + 1)
                start(*place, sub, onward, receipt(dim, o, sign, step + 1, sub), away(dim, sign))
            return not last or direct or sign < 0

        for time in range(n1 // 2 + n2 // 2 + 1):
            if time == 0:
                question_0()
                wout_0()
            for sub in range(SUBS):
                if time == 0:
                    spread(1, 0, sub)
                    spread(2, 0, sub)
                    hand_over(0, 0, sub)
                elif time <= n1 // 2:
                    for sign in (1, -1):
                        if arrive(1, 0, sign, time, sub):
                            spread(2, -sign * time, sub)
                            hand_over(-sign * time, 0, sub)
                if time <= YN // 2 and sub == 0:
                    rows_step(time)
                for step in range(1, n2 // 2 + 1):
                    o = time - step
                    if 0 <= o <= n1 // 2:
                        for signed in (o,) if o in (0, n1 // 2) else (o, -o):
                            for sign in (1, -1):
                                if arrive(2, signed, sign, step, sub):
                                    hand_over(signed, -sign * step, sub)
            if time == 1:
                question_1()
            if time == 2:
                question_2()
            if time == 3:
                question_3()
            if time == 4:
                wout_1()
        return sends

    sends = [None, None]
    for role in (0, 1):

        @pl.when(core == role)
        def _():
            sends[role] = weights(role)

    for chip in range(ZN * XN):
        for sub in range(SUBS):
            sl = wg.at[chip * 2 + (1 - core), pl.ds(64 // SUBS * sub, 64 // SUBS)]
            remote(sl, sl, ring_send.at[0], sib_recv.at[chip, sub], sibling).wait_recv()
    wout_2()

    def project(low, high):
        squares = jnp.zeros((high - low, 128), F32)
        for d in range(YN):
            block = xg[d, low:high, :].astype(F32)
            block = block * block
            squares += block[:, 0:128] + block[:, 128:256] + block[:, 256:384] + block[:, 384:512]
        inverse = lax.rsqrt(jnp.sum(squares, axis=1, keepdims=True) * (1.0 / (512 * YN)) + NORM_EPSILON)
        for d in range(YN):
            scale = jnp.concatenate([gain[4 * d + part : 4 * d + part + 1, :] for part in range(4)], axis=1)
            xn[low:high, 512 * d : 512 * d + 512] = (xg[d, low:high, :].astype(F32) * inverse * scale).astype(BF16)
        totals = []
        for part in range(3):
            weight = wg[:, :, 256 * part : 256 * part + 256].reshape(4096, 256)
            totals.append(jnp.dot(xn[low:high, :], weight, preferred_element_type=F32).astype(BF16))
        return totals

    first_rows = project(0, 192)
    question_end(1)
    last_rows = project(192, 224)
    queries, keys, values = (jnp.concatenate(both, axis=0) for both in zip(first_rows, last_rows))

    def pair_of(index):
        return jnp.where(index < 192, index // 64, jnp.minimum((index - 192) // 8, CAP - 1))

    row_ids = lax.broadcasted_iota(jnp.int32, (224, 224), 0)
    col_ids = lax.broadcasted_iota(jnp.int32, (224, 224), 1)
    col_pair = pair_of(col_ids)
    length = jnp.where(col_pair == 0, length_of[0], jnp.where(col_pair == 1, length_of[1], length_of[2]))
    token = col_ids - 192 - 8 * col_pair
    live = (pair_of(row_ids) == col_pair) & (token < length)

    def ctx_copy(part, k, source, half):
        if half is None:
            sl = ctxg.at[wrap(source, YN), part]
        else:
            sl = ctxg.at[wrap(source, YN), part, pl.ds(112 * half, 112)]
        return sl

    def ctx_near(part, k):
        sl = ctx_copy(part, k, y, None)
        return remote(sl, sl, cx_s.at[part, k], cx_r.at[part, k], at_y(k - 3))

    for part in range(2):
        outs = []
        for h in (2 * part, 2 * part + 1):
            sl = slice(64 * h, 64 * h + 64)
            scores = dot_nt(queries[:, sl], keys[:, sl]) * (HEAD_DIM**-0.5)
            weight = jnp.where(live, jnp.exp(scores), 0.0)
            prob = (weight / jnp.sum(weight, axis=1, keepdims=True)).astype(BF16)
            outs.append(jnp.dot(prob, values[:, sl], preferred_element_type=F32))
        ctxg[y, part] = jnp.concatenate(outs, axis=1).astype(BF16)
        for k in (-2, 2, -1, 1):
            ctx_near(part, k + 3).start()

    def ctx_recv(part, k, half=None):
        sl = ctx_copy(part, k, y - k, half)
        return sl

    def ctx_wait(part, k, half=None):
        sl = ctx_recv(part, k, half)
        slot = k + 3 if abs(k) <= 2 else {3: 6, -3: 7, 4: 8, -4: 9}[k]
        remote(sl, sl, cx_s.at[part, 0], cx_r.at[part, slot], at_y(1)).wait_recv()

    def ctx_forward(part, sign):
        sl = ctx_copy(part, 0, y - 2 * sign, None)
        slot = 6 if sign > 0 else 7
        remote(sl, sl, cx_s.at[part, slot], cx_r.at[part, slot], at_y(sign)).start()
        half = 0 if sign > 0 else 1
        sl = ctx_copy(part, 0, y - 2 * sign, half)
        slot = 8 if sign > 0 else 9
        remote(sl, sl, cx_s.at[part, slot], cx_r.at[part, slot], at_y(2 * sign)).start()

    load_k.wait()
    question_end(0)
    lane_head = lax.broadcasted_iota(jnp.int32, (8, 256), 1) // 64
    for g in range(YN):
        asked = dqg[g].astype(F32)
        blocks = []
        for c in range(CAP):
            for h in range(4):
                blocks.append(jnp.where(lane_head == h, asked[8 * c : 8 * c + 8], 0.0))
        spread = jnp.concatenate(blocks, axis=0).astype(BF16)
        product = dot_nt(spread, dwk[:, 256 * g : 256 * g + 256]).astype(BF16)
        for c in range(CAP):
            dqp[c, 32 * g : 32 * g + 32, :] = product[32 * c : 32 * c + 32]

    for part in range(2):
        for sign in (1, -1):
            ctx_wait(part, 2 * sign)
            ctx_forward(part, sign)
    wout_3()
    for part in range(2):
        for sign in (1, -1):
            ctx_wait(part, sign)
            ctx_wait(part, 3 * sign)
            ctx_wait(part, 4 * sign, 0 if sign > 0 else 1)
    w_s(1 - core).wait_recv()

    attended = jnp.zeros((224, 512), F32)
    for d in range(YN):
        context = jnp.concatenate([ctxg[d, 0], ctxg[d, 1]], axis=1)
        weight = jnp.concatenate(
            [wot[((r % 2) * XN + r // 2) * ZN + d] for r in range(8)], axis=0
        )
        attended += dot_nt(context, weight)
    enc[...] = (xg[y].astype(F32) + attended).astype(BF16)

    for c in range(CAP):
        ekeys[c, 0:64, :] = enc[64 * c : 64 * c + 64, :]
        ekeys[c, 64:96, :] = enc[192:224, :]
        ekeys[c, 96:128, :] = jnp.zeros((32, 512), BF16)
        part = dot_nt(dqp[c], ekeys[c]).astype(BF16)
        for g in range(YN):
            cs[g, 32 * c : 32 * c + 32, :] = part[32 * g : 32 * g + 32]

    def scatter(src, dst, send, recv, k):
        return remote(src.at[wrap(y + k, YN)], dst.at[y], send.at[k], recv.at[k], at_y(k))

    def scattered(src, dst, send, recv, k):
        sl = dst.at[wrap(y - k, YN)]
        return remote(sl, sl, send.at[k], recv.at[k], at_y(k))

    for k in FAR_FIRST:
        scatter(cs, cr, a_s, a_r, k).start()
    for k in FAR_FIRST:
        scattered(cs, cr, a_s, a_r, k).wait_recv()
    total = cs[y].astype(F32)
    for k in range(1, 8):
        total += cr[wrap(y - k, YN)].astype(F32)
    lanes = lax.broadcasted_iota(jnp.int32, (32, 128), 1)
    masks = []
    for c in range(CAP):
        spot = lanes - 64 - 8 * c
        masks.append((lanes < 64) | ((spot >= 0) & (spot < length_of[c])))
    cross = jnp.concatenate(
        [jnp.where(masks[c], jnp.exp(total[32 * c : 32 * c + 32] * (HEAD_DIM**-0.5)), 0.0) for c in range(CAP)], axis=0
    )
    den = jnp.sum(cross, axis=1, keepdims=True)
    cwg[y] = cross.astype(BF16)
    sl = cwg.at[y]
    for k in FAR_FIRST:
        remote(sl, sl, b_s.at[k], b_r.at[k], at_y(k)).start()
    load_v.wait()
    for k in FAR_FIRST:
        scattered(cwg, cwg, b_s, b_r, k).wait_recv()

    mixed = []
    for c in range(CAP):
        cw = jnp.concatenate([cwg[g, 32 * c : 32 * c + 32] for g in range(YN)], axis=0)
        mixed.append(jnp.dot(cw, ekeys[c], preferred_element_type=F32).astype(BF16))
    for g in range(YN):
        left = jnp.concatenate([mixed[c][32 * g : 32 * g + 32] for c in range(CAP)], axis=0)
        product = jnp.dot(left, dwv[:, 256 * g : 256 * g + 256], preferred_element_type=F32)
        rows = []
        for c in range(CAP):
            row = jnp.zeros((8, 256), F32)
            for h in range(4):
                low = 32 * c + 8 * h
                row += jnp.where(lane_head == h, product[low : low + 8], 0.0)
            rows.append(row)
        rows.append(jnp.zeros((8, 256), F32))
        ns[g] = jnp.concatenate(rows, axis=0).astype(BF16)
    for k in FAR_FIRST:
        scatter(ns, nr, n_s, n_r, k).start()
    for k in FAR_FIRST:
        scattered(ns, nr, n_s, n_r, k).wait_recv()
    num = ns[y].astype(F32)
    for k in range(1, 8):
        num += nr[wrap(y - k, YN)].astype(F32)

    packed = []
    for c in range(CAP):
        wide = jnp.zeros((8, 256), F32)
        for h in range(4):
            low = 32 * c + 8 * h
            wide = jnp.where(lane_head == h, den[low : low + 8], wide)
        packed.append(jnp.concatenate([num[8 * c : 8 * c + 8], wide], axis=0))
    for spot in range(8):
        for zz in range(ZN):
            question = zz * 8 + spot
            value = jnp.zeros((16, 256), F32)
            for c in range(CAP):
                value += jnp.where(asking[c] == question, packed[c], 0.0)
            t1s[spot, zz] = value.astype(BF16)
    for k in FAR_FIRST:
        remote(t1s.at[lax.rem(r8 + k, 8)], t1r.at[r8], f_s.at[k], f_r.at[k], at_xc(k)).start()
    for k in FAR_FIRST:
        sl = t1r.at[lax.rem(r8 + 8 - k, 8)]
        remote(sl, sl, f_s.at[k], f_r.at[k], at_xc(k)).wait_recv()
    gathered = t1s[r8].astype(F32)
    for k in range(1, 8):
        gathered += t1r[lax.rem(r8 + 8 - k, 8)].astype(F32)
    t2s[...] = gathered.astype(BF16)
    for k in FAR_FIRST:
        remote(t2s.at[wrap(z + k, ZN)], t2r.at[z], h_s.at[k], h_r.at[k], at_z(k)).start()
    for k in FAR_FIRST:
        sl = t2r.at[wrap(z - k, ZN)]
        remote(sl, sl, h_s.at[k], h_r.at[k], at_z(k)).wait_recv()
    answer = t2s[z].astype(F32)
    for k in range(1, 8):
        answer += t2r[wrap(z - k, ZN)].astype(F32)
    out[0] = (answer[0:8] / answer[8:16]).astype(BF16)

    for role in (0, 1):

        @pl.when(core == role)
        def _():
            for number, half in enumerate(sends[role]):
                sl = wg.at[0, pl.ds(0, 64 // SUBS if half is None else 32 // SUBS)]
                remote(sl, sl, ring_send.at[number], sib_recv.at[0, 0], sibling).wait_send()

    @pl.when(has_swap)
    def _():
        w_swap().wait_send()

    q_s(core).wait_send()
    w_s(core).wait_send()
    for k in (1, 2, 3):
        q_x(k, x).wait_send()
        w_x(k, x).wait_send()
    for c in range(CAP):
        for sign in (1, -1):
            for step in range(1, YN // 2 + 1):
                y_copy(c, sign, step, y).wait_send()
    for part in range(2):
        for slot in (1, 2, 4, 5, 6, 7, 8, 9):
            sl = ctx_copy(part, 0, y, None if slot < 8 else 0)
            remote(sl, sl, cx_s.at[part, slot], cx_r.at[part, slot], at_y(1)).wait_send()
    for k in range(1, 8):
        q_z(k, z).wait_send()
        w_z(k, z).wait_send()
        for which in (1, 0):
            q_y(which, k, y).wait_send()
        scatter(cs, cr, a_s, a_r, k).wait_send()
        scatter(cwg, cwg, b_s, b_r, k).wait_send()
        scatter(ns, nr, n_s, n_r, k).wait_send()
        remote(t1s.at[0], t1r.at[0], f_s.at[k], f_r.at[k], at_xc(k)).wait_send()
        remote(t2s.at[0], t2r.at[0], h_s.at[k], h_r.at[k], at_z(k)).wait_send()


def body(
    question_states, passage_cache, norm_gain, enc_wq, enc_wk, enc_wv, enc_wo, dec_wk, dec_wv, dec_queries,
    passage_ids, location, question_lengths,
):
    vmem = pl.BlockSpec(memory_space=pltpu.VMEM)
    anywhere = pl.BlockSpec(memory_space=pl.ANY)
    dma = pltpu.SemaphoreType.DMA
    return pl.pallas_call(
        kernel,
        name="step",
        out_shape=jax.ShapeDtypeStruct((1, 8, 256), BF16),
        in_specs=[pl.BlockSpec(memory_space=pltpu.SMEM)] * 3 + [vmem] * 7 + [anywhere] * 2 + [vmem],
        out_specs=vmem,
        scratch_shapes=[
            pltpu.VMEM((64, 64, 768), BF16),
            pltpu.VMEM((64, 64, 256), BF16),
            pltpu.VMEM((64, 256), BF16),
            pltpu.VMEM((8, 224, 512), BF16),
            pltpu.VMEM((64, 16, 384), BF16),
            pltpu.VMEM((8, 32, 256), BF16),
            pltpu.VMEM((224, 4096), BF16),
            pltpu.VMEM((8, 2, 224, 128), BF16),
            pltpu.VMEM((224, 512), BF16),
            pltpu.VMEM((3, 128, 512), BF16),
            pltpu.VMEM((3, 256, 512), BF16),
            pltpu.VMEM((8, 96, 128), BF16),
            pltpu.VMEM((8, 96, 128), BF16),
            pltpu.VMEM((8, 96, 128), BF16),
            pltpu.VMEM((8, 32, 256), BF16),
            pltpu.VMEM((8, 32, 256), BF16),
            pltpu.VMEM((8, 8, 16, 256), BF16),
            pltpu.VMEM((8, 8, 16, 256), BF16),
            pltpu.VMEM((8, 16, 256), BF16),
            pltpu.VMEM((8, 16, 256), BF16),
            pltpu.VMEM((512, 2048), BF16),
            pltpu.VMEM((512, 2048), BF16),
            dma((2,)),
            dma((80 * SUBS,)),
            dma((2, 5, SUBS)),
            dma((8, 2, 5, SUBS)),
            dma((32, SUBS)),
            dma((3, 2, 5)),
            dma((3, 2, 5)),
            dma((8,)), dma((8,)), dma((4,)), dma((4,)), dma((1,)), dma((1,)), dma((2, 8)), dma((2, 8)),
            dma((1,)), dma((1,)), dma((8,)), dma((8,)), dma((4,)), dma((4,)), dma((1,)), dma((1,)),
            dma((2, 10)), dma((2, 10)),
            dma((8,)), dma((8,)), dma((8,)), dma((8,)), dma((8,)), dma((8,)), dma((8,)), dma((8,)), dma((8,)), dma((8,)),
        ],
        compiler_params=pltpu.CompilerParams(
            collective_id=0, has_side_effects=True, vmem_limit_bytes=56 * 2**20
        ),
    )(
        passage_ids.T, location, question_lengths, question_states, passage_cache, norm_gain.reshape(32, 128),
        enc_wq, enc_wk, enc_wv, enc_wo.T,
        dec_wk, dec_wv, dec_queries,
    )


def solution(mesh):
    in_specs = (
        P("mem", None, "dec"),
        P("mem", None, "dec"),
        P(),
        P("mem", "dec"),
        P("mem", "dec"),
        P("mem", "dec"),
        P("dec", "mem"),
        P("dec", None),
        P("dec", None),
        P("mem", None, "dec"),
        P(),
        P(),
        P(),
    )
    return jax.shard_map(body, mesh=mesh, in_specs=in_specs, out_specs=P("mem", None, "dec"), check_vma=False)
```

```python
import functools

import jax
import jax.numpy as jnp
from jax import lax
from jax.experimental import pallas as pl
from jax.experimental.pallas import tpu as pltpu
from jax.sharding import PartitionSpec as P

MESH = pl.DeviceIdType.MESH
BF16, F32 = jnp.bfloat16, jnp.float32
ZN, XN, YN = 8, 4, 8
CAP = 3
MODES = (("hybrid", "ring"), ("direct", "ring"))
(G_QZ, G_QX, G_QS, G_QY, G_DY, G_WP, G_WZ, G_WX, G_WS, G_CTX, G_A, G_B, G_N, G_F, G_H, G_RING, G_ROWS) = range(17)
HEAD_DIM = 64
NORM_EPSILON = 1e-06
FAR_FIRST = (4, 3, 5, 2, 6, 1, 7)
NT = (((1,), (1,)), ((), ()))


def wrap(value, size):
    return lax.rem(value + size, size)


def dot_nt(a, b):
    return lax.dot_general(a, b, NT, preferred_element_type=F32)


def kernel(
    ids_in, rows_in, lengths_in, qs_in, cache_in, gain_in, wq_in, wk_in, wv_in, wo_in, dwk_in, dwv_in, dq_in,
    out,
    ids, rows_of, lengths, qs, cache, gain, dq,
    wg, wot, wot_own, xg, qg, dqg, xn, ctxg, enc, ekeys, dqp, cs, cr, cwg, ns, nr, t1r, t2s, t2r, dwk, dwv,
    load_sem, ring1, ring2, sib_recv, rows_recv, ctx_sem, sent, got,
):
    m = lax.axis_index("mem")
    y = lax.axis_index("dec")
    z = m // (2 * XN)
    x = lax.rem(m // 2, XN)
    core = lax.rem(m, 2)
    r8 = lax.rem(m, 8)

    def device(zz, xx, cc, yy):
        return ((zz * XN + xx) * 2 + cc, yy)

    def at_z(k):
        return device(wrap(z + k, ZN), x, core, y)

    def at_x(k):
        return device(z, wrap(x + k, XN), core, y)

    def at_y(k):
        return device(z, x, core, wrap(y + k, YN))

    def at_xc(k):
        other = lax.rem(r8 + k, 8)
        return (z * 8 + other, y)

    sibling = device(z, x, 1 - core, y)
    swap = (8 * y + r8, z)
    has_swap = z != y

    def remote(src, dst, send, recv, to):
        return pltpu.make_async_remote_copy(
            src_ref=src, dst_ref=dst, send_sem=send, recv_sem=recv, device_id=to, device_id_type=MESH
        )

    def all_sent(group, ref):
        remote(ref, ref, sent.at[group], got.at[group], sibling).wait_send()

    def all_got(group, ref):
        remote(ref, ref, sent.at[group], got.at[group], sibling).wait_recv()

    barrier = pltpu.get_barrier_semaphore()
    for k in range(1, 8):
        pl.semaphore_signal(barrier, inc=1, device_id=at_y(k), device_id_type=MESH)
        pl.semaphore_signal(barrier, inc=1, device_id=at_z(k), device_id_type=MESH)
        pl.semaphore_signal(barrier, inc=1, device_id=at_xc(k), device_id_type=MESH)

    @pl.when(has_swap)
    def _():
        pl.semaphore_signal(barrier, inc=1, device_id=swap, device_id_type=MESH)

    loads = [
        pltpu.make_async_copy(source, target, load_sem.at[number])
        for number, (source, target) in enumerate(
            [
                (ids_in, ids), (rows_in, rows_of), (lengths_in, lengths),
                (cache_in, cache), (qs_in, qs), (dq_in, dq), (wo_in, wot_own), (gain_in, gain),
                (wq_in, wg.at[m, :, pl.ds(0, 256)]),
                (wk_in, wg.at[m, :, pl.ds(256, 256)]),
                (wv_in, wg.at[m, :, pl.ds(512, 256)]),
                (dwk_in, dwk), (dwv_in, dwv),
            ]
        )
    ]
    for load in loads:
        load.start()
    load_k, load_v = loads[11:]

    def look(index, found):
        count, slots, asking = found
        question, pick = index // 2, lax.rem(index, 2)
        place = rows_of[ids[pick, question]] - 4 * m
        hit = (place >= 0) & (place < 4)
        taken = [hit & (count == c) for c in range(CAP)]
        return (
            count + jnp.where(hit, 1, 0),
            tuple(jnp.where(taken[c], place, slots[c]) for c in range(CAP)),
            tuple(jnp.where(taken[c], question, asking[c]) for c in range(CAP)),
        )

    for load in loads[:3]:
        load.wait()
    zero, none = jnp.int32(0), jnp.int32(-1)
    _, slots, asking = lax.fori_loop(0, 2 * 64, look, (zero, (zero,) * CAP, (none,) * CAP), unroll=8)
    asked_question = [jnp.maximum(asking[c], 0) for c in range(CAP)]
    length_of = [lengths[asked_question[c]] for c in range(CAP)]
    for load in loads[3:11]:
        load.wait()
    for c in range(CAP):
        xg[y, 64 * c : 64 * c + 64, :] = cache[slots[c]]

    first = qs[0].astype(F32)
    second = jnp.concatenate([first[:, 384:512], dq[0].astype(F32)], axis=1)
    own_q = (core * XN + x) * ZN + z
    qg[own_q] = jnp.concatenate([first[:, 0:384], second], axis=0).astype(BF16)

    @pl.when(jnp.logical_not(has_swap))
    def _():
        wot[own_q] = wot_own[...]

    @pl.when(has_swap)
    def _():
        pl.semaphore_wait(barrier, 22)

    @pl.when(jnp.logical_not(has_swap))
    def _():
        pl.semaphore_wait(barrier, 21)

    def q_z(k, source):
        sl = qg.at[(core * XN + x) * ZN + wrap(source, ZN)]
        return remote(sl, sl, sent.at[G_QZ], got.at[G_QZ], at_z(k))

    def q_x(k, source):
        sl = qg.at[pl.ds((core * XN + wrap(source, XN)) * ZN, ZN)]
        return remote(sl, sl, sent.at[G_QX], got.at[G_QX], at_x(k))

    def q_s(cc):
        sl = qg.at[pl.ds(cc * (XN * ZN), XN * ZN)]
        return remote(sl, sl, sent.at[G_QS], got.at[G_QS], sibling)

    def q_y(which, k, source):
        sl = (dqg.at[wrap(source, YN)], xg.at[wrap(source, YN), pl.ds(192, 32)])[which]
        group = (G_DY, G_QY)[which]
        return remote(sl, sl, sent.at[group], got.at[group], at_y(k))

    def question_0():
        for k in FAR_FIRST:
            q_z(k, z).start()

    def question_1():
        all_got(G_QZ, qg.at[pl.ds(0, 7)])
        for k in (2, 1, 3):
            q_x(k, x).start()

    def question_2():
        all_got(G_QX, qg.at[pl.ds(0, 24)])
        q_s(core).start()

    def question_3():
        q_s(1 - core).wait_recv()
        rows, queries = [], []
        for c in range(CAP):
            q = asked_question[c]
            asked = qg[(lax.rem(q, 2) * XN + lax.rem(q // 2, XN)) * ZN + q // (2 * XN)].astype(F32)
            rows.append(jnp.concatenate([asked[0:8], asked[8:16, 0:128]], axis=1))
            queries.append(asked[8:16, 128:384])
        rows.append(jnp.zeros((8, 512), F32))
        queries.append(jnp.zeros((8, 256), F32))
        xg[y, 192:224, :] = jnp.concatenate(rows, axis=0).astype(BF16)
        dqg[y] = jnp.concatenate(queries, axis=0).astype(BF16)
        for which in (1, 0):
            for k in FAR_FIRST:
                q_y(which, k, y).start()

    def question_end(which):
        if which:
            all_got(G_QY, xg.at[0])
        else:
            all_got(G_DY, dqg.at[pl.ds(0, 7)])

    def w_swap():
        return remote(wot_own, wot.at[(lax.rem(r8, 2) * XN + r8 // 2) * ZN + y], sent.at[G_WP], got.at[G_WP], swap)

    def w_z(k, source):
        sl = wot.at[(core * XN + x) * ZN + wrap(source, ZN)]
        return remote(sl, sl, sent.at[G_WZ], got.at[G_WZ], at_z(k))

    def w_x(k, source):
        sl = wot.at[pl.ds((core * XN + wrap(source, XN)) * ZN, ZN)]
        return remote(sl, sl, sent.at[G_WX], got.at[G_WX], at_x(k))

    def w_s(cc):
        sl = wot.at[pl.ds(cc * (XN * ZN), XN * ZN)]
        return remote(sl, sl, sent.at[G_WS], got.at[G_WS], sibling)

    def wout_0():
        @pl.when(has_swap)
        def _():
            w_swap().start()

    def wout_1():
        @pl.when(has_swap)
        def _():
            w_swap().wait_recv()

        for k in FAR_FIRST:
            w_z(k, z).start()

    def wout_2():
        all_got(G_WZ, wot.at[pl.ds(0, 7)])
        for k in (2, 1, 3):
            w_x(k, x).start()

    def wout_3():
        all_got(G_WX, wot.at[pl.ds(0, 24)])
        w_s(core).start()

    def y_copy(c, sign, step, source):
        if step < YN // 2:
            sl = xg.at[wrap(source, YN), pl.ds(64 * c, 64)]
        else:
            sl = xg.at[wrap(source, YN), pl.ds(64 * c + (0 if sign > 0 else 32), 32)]
        d = 0 if sign > 0 else 1
        return remote(sl, sl, sent.at[G_ROWS], rows_recv.at[c, d, step], at_y(sign))

    def rows_step(step):
        for c in range(CAP):
            for sign in (1, -1):
                if step > 0:
                    y_copy(c, sign, step, y - sign * step).wait_recv()
                if step < YN // 2:
                    y_copy(c, sign, step + 1, y - sign * step).start()

    def weights(role):
        n1, n2 = (ZN, XN) if role == 0 else (XN, ZN)
        i1, i2 = (z, x) if role == 0 else (x, z)
        mode_1, mode_2 = MODES[role]

        def away(dim, distance):
            return at_z(distance) if (dim == 1) == (role == 0) else at_x(distance)

        def chip(o, p):
            a, b = wrap(i1 + o, n1), wrap(i2 + p, n2)
            return a * XN + b if role == 0 else b * XN + a

        def copy(o, p, half, recv, to):
            index = chip(o, p) * 2 + role
            sl = wg.at[index] if half is None else wg.at[index, pl.ds(32 * half, 32)]
            return remote(sl, sl, sent.at[G_RING], recv, to)

        def hand_over(o, p):
            copy(o, p, None, sib_recv.at[0], sibling).start()

        def way(sign):
            return 0 if sign > 0 else 1

        def receipt(dim, o, sign, step):
            return ring1.at[way(sign), step] if dim == 1 else ring2.at[o % n1, way(sign), step]

        def travel(dim):
            return (n1, mode_1) if dim == 1 else (n2, mode_2)

        def half_at(dim, sign, step):
            count, mode = travel(dim)
            return way(sign) if step == count // 2 and mode != "direct" else None

        def spread(dim, o):
            count, mode = travel(dim)
            if mode == "ring":
                steps = (1,)
            elif mode == "hybrid":
                steps = (2, 1)
            else:
                steps = range(1, count // 2 + 1)
            for step in steps:
                for sign in (1, -1) if mode != "direct" or step < count // 2 else (1,):
                    half = half_at(dim, sign, step)
                    copy(o, 0, half, receipt(dim, o, sign, step), away(dim, sign * step)).start()

        def arrive(dim, o, sign, step):
            count, mode = travel(dim)
            last = step == count // 2
            if mode == "direct" and last and sign < 0:
                return False
            place = (-sign * step, 0) if dim == 1 else (o, -sign * step)
            copy(*place, half_at(dim, sign, step), receipt(dim, o, sign, step), away(dim, sign)).wait_recv()
            if mode == "ring" and not last:
                onward = half_at(dim, sign, step + 1)
                copy(*place, onward, receipt(dim, o, sign, step + 1), away(dim, sign)).start()
            if mode == "hybrid" and step == 2:
                copy(*place, None, receipt(dim, o, sign, 3), away(dim, sign)).start()
                copy(*place, way(sign), receipt(dim, o, sign, 4), away(dim, 2 * sign)).start()
            return not last or mode == "direct" or sign < 0

        def when(mode, step):
            return {"ring": step, "direct": min(step, 1), "hybrid": (step + 1) // 2}[mode]

        def order(mode, count):
            return (2, 1, 3, 4) if mode == "hybrid" else range(1, count // 2 + 1)

        events = [(when(mode_1, step), 0, 1, step, 0) for step in order(mode_1, n1)]
        for o in range(n1 // 2 + 1):
            events += [(when(mode_1, o) + when(mode_2, step), 1, 2, step, o) for step in order(mode_2, n2)]
        events.sort(key=lambda event: event[:2])

        question_0()
        wout_0()
        spread(1, 0)
        spread(2, 0)
        hand_over(0, 0)
        rows_step(0)
        after = {1: question_1, 2: question_2, 3: question_3, 4: wout_1}
        for time in range(1, max(4, events[-1][0]) + 1):
            now = [event for event in events if event[0] == time]
            for _, _, dim, step, o in now:
                if dim == 1:
                    for sign in (1, -1):
                        if arrive(1, 0, sign, step):
                            spread(2, -sign * step)
                            hand_over(-sign * step, 0)
            if time <= YN // 2:
                rows_step(time)
            for _, _, dim, step, o in now:
                if dim == 2:
                    for signed in (o,) if o in (0, n1 // 2) else (o, -o):
                        for sign in (1, -1):
                            if arrive(2, signed, sign, step):
                                hand_over(signed, -sign * step)
            if time in after:
                after[time]()

    for role in (0, 1):

        @pl.when(core == role)
        def _():
            weights(role)

    question_end(1)
    squares = jnp.zeros((224, 128), F32)
    for d in range(YN):
        block = xg[d].astype(F32)
        block = block * block
        squares += block[:, 0:128] + block[:, 128:256] + block[:, 256:384] + block[:, 384:512]
    inverse = lax.rsqrt(jnp.sum(squares, axis=1, keepdims=True) * (1.0 / (512 * YN)) + NORM_EPSILON)
    for d in range(YN):
        scale = jnp.concatenate([gain[4 * d + part : 4 * d + part + 1, :] for part in range(4)], axis=1)
        xn[:, 512 * d : 512 * d + 512] = (xg[d].astype(F32) * inverse * scale).astype(BF16)

    remote(wg.at[pl.ds(0, 32)], wg.at[pl.ds(0, 32)], sent.at[G_RING], sib_recv.at[0], sibling).wait_recv()
    wout_2()
    queries, keys, values = (
        jnp.dot(
            xn[...], wg[:, :, 256 * part : 256 * part + 256].reshape(4096, 256), preferred_element_type=F32
        ).astype(BF16)
        for part in range(3)
    )

    def pair_of(index):
        return jnp.where(index < 192, index // 64, jnp.minimum((index - 192) // 8, CAP - 1))

    row_ids = lax.broadcasted_iota(jnp.int32, (224, 224), 0)
    col_ids = lax.broadcasted_iota(jnp.int32, (224, 224), 1)
    col_pair = pair_of(col_ids)
    length = jnp.where(col_pair == 0, length_of[0], jnp.where(col_pair == 1, length_of[1], length_of[2]))
    token = col_ids - 192 - 8 * col_pair
    live = (pair_of(row_ids) == col_pair) & (token < length)

    def ctx_copy(part, k, source, half):
        if half is None:
            sl = ctxg.at[wrap(source, YN), part]
        else:
            sl = ctxg.at[wrap(source, YN), part, pl.ds(112 * half, 112)]
        return sl

    def ctx_near(part, k):
        sl = ctx_copy(part, k, y, None)
        return remote(sl, sl, sent.at[G_CTX], ctx_sem.at[part, k], at_y(k - 3))

    for part in range(2):
        outs = []
        for h in (2 * part, 2 * part + 1):
            sl = slice(64 * h, 64 * h + 64)
            scores = dot_nt(queries[:, sl], keys[:, sl]) * (HEAD_DIM**-0.5)
            weight = jnp.where(live, jnp.exp(scores), 0.0)
            prob = (weight / jnp.sum(weight, axis=1, keepdims=True)).astype(BF16)
            outs.append(jnp.dot(prob, values[:, sl], preferred_element_type=F32))
        ctxg[y, part] = jnp.concatenate(outs, axis=1).astype(BF16)
        for k in (-2, 2, -1, 1):
            ctx_near(part, k + 3).start()

    def ctx_recv(part, k, half=None):
        sl = ctx_copy(part, k, y - k, half)
        return sl

    def ctx_wait(part, k, half=None):
        sl = ctx_recv(part, k, half)
        slot = k + 3 if abs(k) <= 2 else {3: 6, -3: 7, 4: 8, -4: 9}[k]
        remote(sl, sl, sent.at[G_CTX], ctx_sem.at[part, slot], at_y(1)).wait_recv()

    def ctx_forward(part, sign):
        sl = ctx_copy(part, 0, y - 2 * sign, None)
        slot = 6 if sign > 0 else 7
        remote(sl, sl, sent.at[G_CTX], ctx_sem.at[part, slot], at_y(sign)).start()
        half = 0 if sign > 0 else 1
        sl = ctx_copy(part, 0, y - 2 * sign, half)
        slot = 8 if sign > 0 else 9
        remote(sl, sl, sent.at[G_CTX], ctx_sem.at[part, slot], at_y(2 * sign)).start()

    load_k.wait()
    question_end(0)
    lane_head = lax.broadcasted_iota(jnp.int32, (8, 256), 1) // 64
    for g in range(YN):
        asked = dqg[g].astype(F32)
        blocks = []
        for c in range(CAP):
            for h in range(4):
                blocks.append(jnp.where(lane_head == h, asked[8 * c : 8 * c + 8], 0.0))
        spread = jnp.concatenate(blocks, axis=0).astype(BF16)
        product = dot_nt(spread, dwk[:, 256 * g : 256 * g + 256]).astype(BF16)
        for c in range(CAP):
            dqp[c, 32 * g : 32 * g + 32, :] = product[32 * c : 32 * c + 32]

    all_sent(G_RING, wg.at[pl.ds(0, 63)])
    all_sent(G_ROWS, xg.at[pl.ds(0, 6)])
    all_sent(G_QZ, qg.at[pl.ds(0, 7)])
    all_sent(G_QX, qg.at[pl.ds(0, 24)])
    all_sent(G_QS, qg.at[pl.ds(0, 32)])
    all_sent(G_QY, xg.at[0])
    all_sent(G_DY, dqg.at[pl.ds(0, 7)])
    all_sent(G_WZ, wot.at[pl.ds(0, 7)])

    @pl.when(has_swap)
    def _():
        w_swap().wait_send()

    for part in range(2):
        for sign in (1, -1):
            ctx_wait(part, 2 * sign)
            ctx_forward(part, sign)
    wout_3()
    for part in range(2):
        for sign in (1, -1):
            ctx_wait(part, sign)
            ctx_wait(part, 3 * sign)
            ctx_wait(part, 4 * sign, 0 if sign > 0 else 1)
    w_s(1 - core).wait_recv()

    attended = jnp.zeros((224, 512), F32)
    for d in range(YN):
        context = jnp.concatenate([ctxg[d, 0], ctxg[d, 1]], axis=1)
        weight = jnp.concatenate(
            [wot[((r % 2) * XN + r // 2) * ZN + d] for r in range(8)], axis=0
        )
        attended += dot_nt(context, weight)
    enc[...] = (xg[y].astype(F32) + attended).astype(BF16)

    for c in range(CAP):
        ekeys[c, 0:64, :] = enc[64 * c : 64 * c + 64, :]
        ekeys[c, 64:96, :] = enc[192:224, :]
        ekeys[c, 96:128, :] = jnp.zeros((32, 512), BF16)
        part = dot_nt(dqp[c], ekeys[c]).astype(BF16)
        for g in range(YN):
            cs[g, 32 * c : 32 * c + 32, :] = part[32 * g : 32 * g + 32]

    def scatter(src, dst, group):
        for k in FAR_FIRST:
            remote(src.at[wrap(y + k, YN)], dst.at[y], sent.at[group], got.at[group], at_y(k)).start()

    seven = pl.ds(0, 7)
    scatter(cs, cr, G_A)
    all_sent(G_WX, wot.at[pl.ds(0, 24)])
    all_sent(G_WS, wot.at[pl.ds(0, 32)])
    all_sent(G_CTX, ctxg.at[seven])
    all_got(G_A, cr.at[seven])
    total = cs[y].astype(F32)
    for k in range(1, 8):
        total += cr[wrap(y - k, YN)].astype(F32)
    lanes = lax.broadcasted_iota(jnp.int32, (32, 128), 1)
    masks = []
    for c in range(CAP):
        spot = lanes - 64 - 8 * c
        masks.append((lanes < 64) | ((spot >= 0) & (spot < length_of[c])))
    cross = jnp.concatenate(
        [jnp.where(masks[c], jnp.exp(total[32 * c : 32 * c + 32] * (HEAD_DIM**-0.5)), 0.0) for c in range(CAP)], axis=0
    )
    den = jnp.sum(cross, axis=1, keepdims=True)
    cwg[y] = cross.astype(BF16)
    sl = cwg.at[y]
    for k in FAR_FIRST:
        remote(sl, sl, sent.at[G_B], got.at[G_B], at_y(k)).start()
    load_v.wait()
    all_sent(G_A, cs.at[seven])
    all_got(G_B, cwg.at[seven])

    mixed = []
    for c in range(CAP):
        cw = jnp.concatenate([cwg[g, 32 * c : 32 * c + 32] for g in range(YN)], axis=0)
        mixed.append(jnp.dot(cw, ekeys[c], preferred_element_type=F32).astype(BF16))
    for g in range(YN):
        left = jnp.concatenate([mixed[c][32 * g : 32 * g + 32] for c in range(CAP)], axis=0)
        product = jnp.dot(left, dwv[:, 256 * g : 256 * g + 256], preferred_element_type=F32)
        rows = []
        for c in range(CAP):
            row = jnp.zeros((8, 256), F32)
            for h in range(4):
                low = 32 * c + 8 * h
                row += jnp.where(lane_head == h, product[low : low + 8], 0.0)
            rows.append(row)
        rows.append(jnp.zeros((8, 256), F32))
        ns[g] = jnp.concatenate(rows, axis=0).astype(BF16)
    scatter(ns, nr, G_N)
    all_sent(G_B, cwg.at[seven])
    all_got(G_N, nr.at[seven])
    num = ns[y].astype(F32)
    for k in range(1, 8):
        num += nr[wrap(y - k, YN)].astype(F32)

    lane = lax.broadcasted_iota(jnp.int32, (8, 128), 1)
    blocks = []
    for c in range(CAP):
        tail = jnp.where(lane == 4, asking[c].astype(F32), 0.0)
        for h in range(4):
            low = 32 * c + 8 * h
            tail = jnp.where(lane == h, den[low : low + 8], tail)
        blocks.append(jnp.concatenate([num[8 * c : 8 * c + 8], tail], axis=1))
    blocks.append(jnp.zeros((8, 384), F32))
    t1r[r8] = jnp.concatenate(blocks, axis=0).astype(BF16)
    sl = t1r.at[r8]
    for k in FAR_FIRST:
        remote(sl, sl, sent.at[G_F], got.at[G_F], at_xc(k)).start()
    all_sent(G_N, ns.at[seven])
    all_got(G_F, t1r.at[seven])
    sums = [jnp.zeros((8, 384), F32) for _ in range(ZN)]
    for source in range(8):
        from_there = t1r[source].astype(F32)
        for c in range(CAP):
            block = from_there[8 * c : 8 * c + 8]
            question = block[:, 260:261]
            for zz in range(ZN):
                here = question == (zz * 8 + r8).astype(F32)
                sums[zz] += jnp.where(here, block, 0.0)
    for zz in range(ZN):
        t2s[zz] = jnp.concatenate([sums[zz], jnp.zeros((8, 384), F32)], axis=0).astype(BF16)
    for k in FAR_FIRST:
        remote(t2s.at[wrap(z + k, ZN)], t2r.at[z], sent.at[G_H], got.at[G_H], at_z(k)).start()
    all_sent(G_F, t1r.at[seven])
    all_got(G_H, t2r.at[seven])
    answer = t2s[z].astype(F32)
    for k in range(1, 8):
        answer += t2r[wrap(z - k, ZN)].astype(F32)
    below = jnp.zeros((8, 256), F32)
    for h in range(4):
        below = jnp.where(lane_head == h, answer[0:8, 256 + h : 257 + h], below)
    out[0] = (answer[0:8, 0:256] / below).astype(BF16)
    all_sent(G_H, t2s.at[seven])


def body(
    question_states, passage_cache, norm_gain, enc_wq, enc_wk, enc_wv, enc_wo, dec_wk, dec_wv, dec_queries,
    passage_ids, location, question_lengths,
):
    vmem = pl.BlockSpec(memory_space=pltpu.VMEM)
    anywhere = pl.BlockSpec(memory_space=pl.ANY)
    dma = pltpu.SemaphoreType.DMA
    return pl.pallas_call(
        kernel,
        name="step",
        out_shape=jax.ShapeDtypeStruct((1, 8, 256), BF16),
        in_specs=[anywhere] * 13,
        out_specs=vmem,
        scratch_shapes=[
            pltpu.SMEM((2, 64), jnp.int32),
            pltpu.SMEM((256,), jnp.int32),
            pltpu.SMEM((64,), jnp.int32),
            pltpu.VMEM((1, 8, 512), BF16),
            pltpu.VMEM((4, 64, 512), BF16),
            pltpu.VMEM((32, 128), F32),
            pltpu.VMEM((1, 8, 256), BF16),
            pltpu.VMEM((64, 64, 768), BF16),
            pltpu.VMEM((64, 64, 256), BF16),
            pltpu.VMEM((64, 256), BF16),
            pltpu.VMEM((8, 224, 512), BF16),
            pltpu.VMEM((64, 16, 384), BF16),
            pltpu.VMEM((8, 32, 256), BF16),
            pltpu.VMEM((224, 4096), BF16),
            pltpu.VMEM((8, 2, 224, 128), BF16),
            pltpu.VMEM((224, 512), BF16),
            pltpu.VMEM((3, 128, 512), BF16),
            pltpu.VMEM((3, 256, 512), BF16),
            pltpu.VMEM((8, 96, 128), BF16),
            pltpu.VMEM((8, 96, 128), BF16),
            pltpu.VMEM((8, 96, 128), BF16),
            pltpu.VMEM((8, 32, 256), BF16),
            pltpu.VMEM((8, 32, 256), BF16),
            pltpu.VMEM((8, 32, 384), BF16),
            pltpu.VMEM((8, 16, 384), BF16),
            pltpu.VMEM((8, 16, 384), BF16),
            pltpu.VMEM((512, 2048), BF16),
            pltpu.VMEM((512, 2048), BF16),
            dma((13,)),
            dma((2, 5)),
            dma((8, 2, 5)),
            dma((1,)),
            dma((3, 2, 5)),
            dma((2, 10)),
            dma((17,)),
            dma((17,)),
        ],
        compiler_params=pltpu.CompilerParams(
            collective_id=0, has_side_effects=True, vmem_limit_bytes=56 * 2**20
        ),
    )(
        passage_ids.T, location, question_lengths, question_states, passage_cache, norm_gain.reshape(32, 128),
        enc_wq, enc_wk, enc_wv, enc_wo.T,
        dec_wk, dec_wv, dec_queries,
    )


def solution(mesh):
    in_specs = (
        P("mem", None, "dec"),
        P("mem", None, "dec"),
        P(),
        P("mem", "dec"),
        P("mem", "dec"),
        P("mem", "dec"),
        P("dec", "mem"),
        P("dec", None),
        P("dec", None),
        P("mem", None, "dec"),
        P(),
        P(),
        P(),
    )
    return jax.shard_map(body, mesh=mesh, in_specs=in_specs, out_specs=P("mem", None, "dec"), check_vma=False)
```

```python
import functools

import jax
import jax.numpy as jnp
from jax import lax
from jax.experimental import pallas as pl
from jax.experimental.pallas import tpu as pltpu
from jax.sharding import PartitionSpec as P

MESH = pl.DeviceIdType.MESH
BF16, F32 = jnp.bfloat16, jnp.float32
ZN, XN, YN = 8, 4, 8
CAP = 3
MODES = (("hybrid", "ring"), ("direct", "ring"))
(G_QZ, G_QX, G_QS, G_QY, G_WP, G_WZ, G_WX, G_WS, G_CTX, G_A, G_B, G_N, G_F, G_H, G_RING, G_SIB, G_ROWS) = range(17)
HEAD_DIM = 64
NORM_EPSILON = 1e-06
FAR_FIRST = (4, 3, 5, 2, 6, 1, 7)
NT = (((1,), (1,)), ((), ()))


def wrap(value, size):
    return lax.rem(value + size, size)


def dot_nt(a, b):
    return lax.dot_general(a, b, NT, preferred_element_type=F32)


def kernel(
    ids_in, rows_in, lengths_in, qs_in, cache_in, gain_in, wq_in, wk_in, wv_in, wo_in, dwk_in, dwv_in, dq_in,
    out,
    ids, rows_of, lengths, qs, cache, gain, dq,
    wg, wot, wot_own, xg, qg, xn, ctxg, enc, ekeys, dqp, cs, cr, cwg, ns, nr, t1r, t2s, t2r, dwk, dwv,
    load_sem, ring1, ring2, sib_recv, rows_recv, ctx_sem, sent, got,
):
    m = lax.axis_index("mem")
    y = lax.axis_index("dec")
    z = m // (2 * XN)
    x = lax.rem(m // 2, XN)
    core = lax.rem(m, 2)
    r8 = lax.rem(m, 8)

    def device(zz, xx, cc, yy):
        return ((zz * XN + xx) * 2 + cc, yy)

    def at_z(k):
        return device(wrap(z + k, ZN), x, core, y)

    def at_x(k):
        return device(z, wrap(x + k, XN), core, y)

    def at_y(k):
        return device(z, x, core, wrap(y + k, YN))

    def at_xc(k):
        other = lax.rem(r8 + k, 8)
        return (z * 8 + other, y)

    sibling = device(z, x, 1 - core, y)
    swap = (8 * y + r8, z)
    has_swap = z != y

    def remote(src, dst, send, recv, to):
        return pltpu.make_async_remote_copy(
            src_ref=src, dst_ref=dst, send_sem=send, recv_sem=recv, device_id=to, device_id_type=MESH
        )

    def all_sent(group, ref):
        remote(ref, ref, sent.at[group], got.at[group], sibling).wait_send()

    def all_got(group, ref):
        remote(ref, ref, sent.at[group], got.at[group], sibling).wait_recv()

    barrier = pltpu.get_barrier_semaphore()
    for k in range(1, 8):
        pl.semaphore_signal(barrier, inc=1, device_id=at_y(k), device_id_type=MESH)
        pl.semaphore_signal(barrier, inc=1, device_id=at_z(k), device_id_type=MESH)
        pl.semaphore_signal(barrier, inc=1, device_id=at_xc(k), device_id_type=MESH)

    @pl.when(has_swap)
    def _():
        pl.semaphore_signal(barrier, inc=1, device_id=swap, device_id_type=MESH)

    loads = [
        pltpu.make_async_copy(source, target, load_sem.at[number])
        for number, (source, target) in enumerate(
            [
                (ids_in, ids), (rows_in, rows_of), (lengths_in, lengths),
                (cache_in, cache), (qs_in, qs), (dq_in, dq), (wo_in, wot_own), (gain_in, gain),
                (wq_in, wg.at[core, m // 2, :, pl.ds(0, 256)]),
                (wk_in, wg.at[core, m // 2, :, pl.ds(256, 256)]),
                (wv_in, wg.at[core, m // 2, :, pl.ds(512, 256)]),
                (dwk_in, dwk), (dwv_in, dwv),
            ]
        )
    ]
    for load in loads:
        load.start()
    load_k, load_v = loads[11:]

    def look(index, found):
        count, slots, asking = found
        question, pick = index // 2, lax.rem(index, 2)
        place = rows_of[ids[pick, question]] - 4 * m
        hit = (place >= 0) & (place < 4)
        taken = [hit & (count == c) for c in range(CAP)]
        return (
            count + jnp.where(hit, 1, 0),
            tuple(jnp.where(taken[c], place, slots[c]) for c in range(CAP)),
            tuple(jnp.where(taken[c], question, asking[c]) for c in range(CAP)),
        )

    for load in loads[:3]:
        load.wait()
    zero, none = jnp.int32(0), jnp.int32(-1)
    _, slots, asking = lax.fori_loop(0, 2 * 64, look, (zero, (zero,) * CAP, (none,) * CAP), unroll=8)
    asked_question = [jnp.maximum(asking[c], 0) for c in range(CAP)]
    length_of = [lengths[asked_question[c]] for c in range(CAP)]
    for load in loads[3:11]:
        load.wait()
    for c in range(CAP):
        xg[y, 64 * c : 64 * c + 64, :] = cache[slots[c]]

    first = qs[0].astype(F32)
    second = jnp.concatenate([first[:, 384:512], dq[0].astype(F32)], axis=1)
    own_q = (core * XN + x) * ZN + z
    qg[own_q] = jnp.concatenate([first[:, 0:384], second], axis=0).astype(BF16)

    @pl.when(jnp.logical_not(has_swap))
    def _():
        wot[own_q] = wot_own[...]

    @pl.when(has_swap)
    def _():
        pl.semaphore_wait(barrier, 22)

    @pl.when(jnp.logical_not(has_swap))
    def _():
        pl.semaphore_wait(barrier, 21)

    def q_z(k, source):
        sl = qg.at[(core * XN + x) * ZN + wrap(source, ZN)]
        return remote(sl, sl, sent.at[G_QZ], got.at[G_QZ], at_z(k))

    def q_x(k, source):
        sl = qg.at[pl.ds((core * XN + wrap(source, XN)) * ZN, ZN)]
        return remote(sl, sl, sent.at[G_QX], got.at[G_QX], at_x(k))

    def q_s(cc):
        sl = qg.at[pl.ds(cc * (XN * ZN), XN * ZN)]
        return remote(sl, sl, sent.at[G_QS], got.at[G_QS], sibling)

    def q_y(k):
        sl = xg.at[y, pl.ds(192, 48)]
        return remote(sl, sl, sent.at[G_QY], got.at[G_QY], at_y(k))

    def question_0():
        for k in FAR_FIRST:
            q_z(k, z).start()

    def question_1():
        all_got(G_QZ, qg.at[pl.ds(0, 7)])
        for k in (2, 1, 3):
            q_x(k, x).start()

    def question_2():
        all_got(G_QX, qg.at[pl.ds(0, 24)])
        q_s(core).start()

    def question_3():
        q_s(1 - core).wait_recv()
        rows, queries = [], []
        for c in range(CAP):
            q = asked_question[c]
            asked = qg[(lax.rem(q, 2) * XN + lax.rem(q // 2, XN)) * ZN + q // (2 * XN)].astype(F32)
            rows.append(jnp.concatenate([asked[0:8], asked[8:16, 0:128]], axis=1))
            queries.append(asked[8:16, 128:384])
        rows.append(jnp.zeros((8, 512), F32))
        queries.append(jnp.zeros((8, 256), F32))
        xg[y, 192:224, :] = jnp.concatenate(rows, axis=0).astype(BF16)
        both = [jnp.concatenate(queries[low : low + 2], axis=0) for low in (0, 2)]
        xg[y, 224:240, :] = jnp.concatenate(both, axis=1).astype(BF16)
        for k in FAR_FIRST:
            q_y(k).start()

    def question_end():
        all_got(G_QY, xg.at[pl.ds(0, 7), pl.ds(192, 48)])

    def w_swap():
        return remote(wot_own, wot.at[(lax.rem(r8, 2) * XN + r8 // 2) * ZN + y], sent.at[G_WP], got.at[G_WP], swap)

    def w_z(k, source):
        sl = wot.at[(core * XN + x) * ZN + wrap(source, ZN)]
        return remote(sl, sl, sent.at[G_WZ], got.at[G_WZ], at_z(k))

    def w_x(k, source):
        sl = wot.at[pl.ds((core * XN + wrap(source, XN)) * ZN, ZN)]
        return remote(sl, sl, sent.at[G_WX], got.at[G_WX], at_x(k))

    def w_s(cc):
        sl = wot.at[pl.ds(cc * (XN * ZN), XN * ZN)]
        return remote(sl, sl, sent.at[G_WS], got.at[G_WS], sibling)

    def wout_0():
        @pl.when(has_swap)
        def _():
            w_swap().start()

    def wout_1():
        @pl.when(has_swap)
        def _():
            w_swap().wait_recv()

        for k in FAR_FIRST:
            w_z(k, z).start()

    def wout_2():
        all_got(G_WZ, wot.at[pl.ds(0, 7)])
        for k in (2, 1, 3):
            w_x(k, x).start()

    def wout_3():
        all_got(G_WX, wot.at[pl.ds(0, 24)])
        w_s(core).start()

    def y_copy(sign, step, source):
        if step < YN // 2:
            sl = xg.at[wrap(source, YN), pl.ds(0, 192)]
        else:
            sl = xg.at[wrap(source, YN), pl.ds(0 if sign > 0 else 96, 96)]
        return remote(sl, sl, sent.at[G_ROWS], rows_recv.at[0 if sign > 0 else 1, step], at_y(sign))

    def rows_step(step):
        for sign in (1, -1):
            if step > 0:
                y_copy(sign, step, y - sign * step).wait_recv()
            if step < YN // 2:
                y_copy(sign, step + 1, y - sign * step).start()

    def weights(role):
        n1, n2 = (ZN, XN) if role == 0 else (XN, ZN)
        i1, i2 = (z, x) if role == 0 else (x, z)
        mode_1, mode_2 = MODES[role]
        landed = {}

        def away(dim, distance):
            return at_z(distance) if (dim == 1) == (role == 0) else at_x(distance)

        def chip(o, p):
            a, b = wrap(i1 + o, n1), wrap(i2 + p, n2)
            return a * XN + b if role == 0 else b * XN + a

        def copy(o, p, half, recv, to):
            index = chip(o, p)
            sl = wg.at[role, index] if half is None else wg.at[role, index, pl.ds(32 * half, 32)]
            return remote(sl, sl, sent.at[G_RING], recv, to)

        def hand_over(o, p):
            far = (o if role == 0 else p) % ZN
            landed[far] = landed.get(far, 0) + 1
            if landed[far] == XN:
                sl = wg.at[role, pl.ds(wrap(z + far, ZN) * XN, XN)]
                remote(sl, sl, sent.at[G_SIB], sib_recv.at[0], sibling).start()

        def way(sign):
            return 0 if sign > 0 else 1

        def receipt(dim, o, sign, step):
            return ring1.at[way(sign), step] if dim == 1 else ring2.at[o % n1, way(sign), step]

        def travel(dim):
            return (n1, mode_1) if dim == 1 else (n2, mode_2)

        def half_at(dim, sign, step):
            count, mode = travel(dim)
            return way(sign) if step == count // 2 and mode != "direct" else None

        def spread(dim, o):
            count, mode = travel(dim)
            if mode == "ring":
                steps = (1,)
            elif mode == "hybrid":
                steps = (2, 1)
            else:
                steps = range(1, count // 2 + 1)
            for step in steps:
                for sign in (1, -1) if mode != "direct" or step < count // 2 else (1,):
                    half = half_at(dim, sign, step)
                    copy(o, 0, half, receipt(dim, o, sign, step), away(dim, sign * step)).start()

        def arrive(dim, o, sign, step):
            count, mode = travel(dim)
            last = step == count // 2
            if mode == "direct" and last and sign < 0:
                return False
            place = (-sign * step, 0) if dim == 1 else (o, -sign * step)
            copy(*place, half_at(dim, sign, step), receipt(dim, o, sign, step), away(dim, sign)).wait_recv()
            if mode == "ring" and not last:
                onward = half_at(dim, sign, step + 1)
                copy(*place, onward, receipt(dim, o, sign, step + 1), away(dim, sign)).start()
            if mode == "hybrid" and step == 2:
                copy(*place, None, receipt(dim, o, sign, 3), away(dim, sign)).start()
                copy(*place, way(sign), receipt(dim, o, sign, 4), away(dim, 2 * sign)).start()
            return not last or mode == "direct" or sign < 0

        def when(mode, step):
            return {"ring": step, "direct": min(step, 1), "hybrid": (step + 1) // 2}[mode]

        def order(mode, count):
            return (2, 1, 3, 4) if mode == "hybrid" else range(1, count // 2 + 1)

        events = [(when(mode_1, step), 0, 1, step, 0) for step in order(mode_1, n1)]
        for o in range(n1 // 2 + 1):
            events += [(when(mode_1, o) + when(mode_2, step), 1, 2, step, o) for step in order(mode_2, n2)]
        events.sort(key=lambda event: event[:2])

        question_0()
        wout_0()
        spread(1, 0)
        spread(2, 0)
        hand_over(0, 0)
        rows_step(0)
        after = {1: question_1, 2: question_2, 3: lambda: (question_3(), wout_1())}
        for time in range(1, max(4, events[-1][0]) + 1):
            now = [event for event in events if event[0] == time]
            for _, _, dim, step, o in now:
                if dim == 1:
                    for sign in (1, -1):
                        if arrive(1, 0, sign, step):
                            spread(2, -sign * step)
                            hand_over(-sign * step, 0)
            if time <= YN // 2:
                rows_step(time)
            for _, _, dim, step, o in now:
                if dim == 2:
                    for signed in (o,) if o in (0, n1 // 2) else (o, -o):
                        for sign in (1, -1):
                            if arrive(2, signed, sign, step):
                                hand_over(signed, -sign * step)
            if time in after:
                after[time]()

    for role in (0, 1):

        @pl.when(core == role)
        def _():
            weights(role)

    wout_2()
    question_end()
    squares = jnp.zeros((224, 128), F32)
    for d in range(YN):
        block = xg[d, 0:224].astype(F32)
        block = block * block
        squares += block[:, 0:128] + block[:, 128:256] + block[:, 256:384] + block[:, 384:512]
    inverse = lax.rsqrt(jnp.sum(squares, axis=1, keepdims=True) * (1.0 / (512 * YN)) + NORM_EPSILON)
    for d in range(YN):
        scale = jnp.concatenate([gain[4 * d + part : 4 * d + part + 1, :] for part in range(4)], axis=1)
        xn[:, 512 * d : 512 * d + 512] = (xg[d, 0:224].astype(F32) * inverse * scale).astype(BF16)

    remote(wg.at[0], wg.at[0], sent.at[G_RING], sib_recv.at[0], sibling).wait_recv()

    def weight_of(low):
        return jnp.concatenate(
            [wg[cc, chip, :, low : low + 256] for chip in range(ZN * XN) for cc in range(2)], axis=0
        )

    queries, keys, values = (
        jnp.dot(xn[...], weight_of(256 * part), preferred_element_type=F32).astype(BF16) for part in range(3)
    )

    def pair_of(index):
        return jnp.where(index < 192, index // 64, jnp.minimum((index - 192) // 8, CAP - 1))

    row_ids = lax.broadcasted_iota(jnp.int32, (224, 224), 0)
    col_ids = lax.broadcasted_iota(jnp.int32, (224, 224), 1)
    col_pair = pair_of(col_ids)
    length = jnp.where(col_pair == 0, length_of[0], jnp.where(col_pair == 1, length_of[1], length_of[2]))
    token = col_ids - 192 - 8 * col_pair
    live = (pair_of(row_ids) == col_pair) & (token < length)

    def ctx_copy(part, k, source, half):
        if half is None:
            sl = ctxg.at[wrap(source, YN), part]
        else:
            sl = ctxg.at[wrap(source, YN), part, pl.ds(112 * half, 112)]
        return sl

    def ctx_near(part, k):
        sl = ctx_copy(part, k, y, None)
        return remote(sl, sl, sent.at[G_CTX], ctx_sem.at[part, k], at_y(k - 3))

    for part in range(2):
        outs = []
        for h in (2 * part, 2 * part + 1):
            sl = slice(64 * h, 64 * h + 64)
            scores = dot_nt(queries[:, sl], keys[:, sl]) * (HEAD_DIM**-0.5)
            weight = jnp.where(live, jnp.exp(scores), 0.0)
            prob = (weight / jnp.sum(weight, axis=1, keepdims=True)).astype(BF16)
            outs.append(jnp.dot(prob, values[:, sl], preferred_element_type=F32))
        ctxg[y, part] = jnp.concatenate(outs, axis=1).astype(BF16)
        for k in (-2, 2, -1, 1):
            ctx_near(part, k + 3).start()

    def ctx_recv(part, k, half=None):
        sl = ctx_copy(part, k, y - k, half)
        return sl

    def ctx_wait(part, k, half=None):
        sl = ctx_recv(part, k, half)
        slot = k + 3 if abs(k) <= 2 else {3: 6, -3: 7, 4: 8, -4: 9}[k]
        remote(sl, sl, sent.at[G_CTX], ctx_sem.at[part, slot], at_y(1)).wait_recv()

    def ctx_forward(part, sign):
        sl = ctx_copy(part, 0, y - 2 * sign, None)
        slot = 6 if sign > 0 else 7
        remote(sl, sl, sent.at[G_CTX], ctx_sem.at[part, slot], at_y(sign)).start()
        half = 0 if sign > 0 else 1
        sl = ctx_copy(part, 0, y - 2 * sign, half)
        slot = 8 if sign > 0 else 9
        remote(sl, sl, sent.at[G_CTX], ctx_sem.at[part, slot], at_y(2 * sign)).start()

    load_k.wait()
    lane_head = lax.broadcasted_iota(jnp.int32, (8, 256), 1) // 64
    for g in range(YN):
        asked = xg[g, 224:240, :].astype(F32)
        asked = jnp.concatenate([asked[:, 0:256], asked[:, 256:512]], axis=0)
        blocks = []
        for c in range(CAP):
            for h in range(4):
                blocks.append(jnp.where(lane_head == h, asked[8 * c : 8 * c + 8], 0.0))
        spread = jnp.concatenate(blocks, axis=0).astype(BF16)
        product = dot_nt(spread, dwk[:, 256 * g : 256 * g + 256]).astype(BF16)
        for c in range(CAP):
            dqp[c, 32 * g : 32 * g + 32, :] = product[32 * c : 32 * c + 32]

    all_sent(G_RING, wg.at[0, pl.ds(0, 31)])
    all_sent(G_SIB, wg.at[0])
    all_sent(G_ROWS, xg.at[pl.ds(0, 7), pl.ds(0, 192)])
    all_sent(G_QZ, qg.at[pl.ds(0, 7)])
    all_sent(G_QX, qg.at[pl.ds(0, 24)])
    all_sent(G_QS, qg.at[pl.ds(0, 32)])
    all_sent(G_QY, xg.at[pl.ds(0, 7), pl.ds(192, 48)])
    all_sent(G_WZ, wot.at[pl.ds(0, 7)])

    @pl.when(has_swap)
    def _():
        w_swap().wait_send()

    for part in range(2):
        for sign in (1, -1):
            ctx_wait(part, 2 * sign)
            ctx_forward(part, sign)
    wout_3()
    for part in range(2):
        for sign in (1, -1):
            ctx_wait(part, sign)
            ctx_wait(part, 3 * sign)
            ctx_wait(part, 4 * sign, 0 if sign > 0 else 1)
    w_s(1 - core).wait_recv()

    attended = jnp.zeros((224, 512), F32)
    for d in range(YN):
        context = jnp.concatenate([ctxg[d, 0], ctxg[d, 1]], axis=1)
        weight = jnp.concatenate(
            [wot[((r % 2) * XN + r // 2) * ZN + d] for r in range(8)], axis=0
        )
        attended += dot_nt(context, weight)
    enc[...] = (xg[y, 0:224].astype(F32) + attended).astype(BF16)

    for c in range(CAP):
        ekeys[c, 0:64, :] = enc[64 * c : 64 * c + 64, :]
        ekeys[c, 64:96, :] = enc[192:224, :]
        ekeys[c, 96:128, :] = jnp.zeros((32, 512), BF16)
        part = dot_nt(dqp[c], ekeys[c]).astype(BF16)
        for g in range(YN):
            cs[g, 32 * c : 32 * c + 32, :] = part[32 * g : 32 * g + 32]

    def scatter(src, dst, group):
        for k in FAR_FIRST:
            remote(src.at[wrap(y + k, YN)], dst.at[y], sent.at[group], got.at[group], at_y(k)).start()

    seven = pl.ds(0, 7)
    scatter(cs, cr, G_A)
    all_sent(G_WX, wot.at[pl.ds(0, 24)])
    all_sent(G_WS, wot.at[pl.ds(0, 32)])
    all_sent(G_CTX, ctxg.at[seven])
    all_got(G_A, cr.at[seven])
    total = cs[y].astype(F32)
    for k in range(1, 8):
        total += cr[wrap(y - k, YN)].astype(F32)
    lanes = lax.broadcasted_iota(jnp.int32, (32, 128), 1)
    masks = []
    for c in range(CAP):
        spot = lanes - 64 - 8 * c
        masks.append((lanes < 64) | ((spot >= 0) & (spot < length_of[c])))
    cross = jnp.concatenate(
        [jnp.where(masks[c], jnp.exp(total[32 * c : 32 * c + 32] * (HEAD_DIM**-0.5)), 0.0) for c in range(CAP)], axis=0
    )
    den = jnp.sum(cross, axis=1, keepdims=True)
    cwg[y] = cross.astype(BF16)
    sl = cwg.at[y]
    for k in FAR_FIRST:
        remote(sl, sl, sent.at[G_B], got.at[G_B], at_y(k)).start()
    load_v.wait()
    all_sent(G_A, cs.at[seven])
    all_got(G_B, cwg.at[seven])

    mixed = []
    for c in range(CAP):
        cw = jnp.concatenate([cwg[g, 32 * c : 32 * c + 32] for g in range(YN)], axis=0)
        mixed.append(jnp.dot(cw, ekeys[c], preferred_element_type=F32).astype(BF16))
    for g in range(YN):
        left = jnp.concatenate([mixed[c][32 * g : 32 * g + 32] for c in range(CAP)], axis=0)
        product = jnp.dot(left, dwv[:, 256 * g : 256 * g + 256], preferred_element_type=F32)
        rows = []
        for c in range(CAP):
            row = jnp.zeros((8, 256), F32)
            for h in range(4):
                low = 32 * c + 8 * h
                row += jnp.where(lane_head == h, product[low : low + 8], 0.0)
            rows.append(row)
        rows.append(jnp.zeros((8, 256), F32))
        ns[g] = jnp.concatenate(rows, axis=0).astype(BF16)
    scatter(ns, nr, G_N)
    all_sent(G_B, cwg.at[seven])
    all_got(G_N, nr.at[seven])
    num = ns[y].astype(F32)
    for k in range(1, 8):
        num += nr[wrap(y - k, YN)].astype(F32)

    lane = lax.broadcasted_iota(jnp.int32, (8, 128), 1)
    blocks = []
    for c in range(CAP):
        tail = jnp.where(lane == 4, asking[c].astype(F32), 0.0)
        for h in range(4):
            low = 32 * c + 8 * h
            tail = jnp.where(lane == h, den[low : low + 8], tail)
        blocks.append(jnp.concatenate([num[8 * c : 8 * c + 8], tail], axis=1))
    blocks.append(jnp.zeros((8, 384), F32))
    t1r[r8] = jnp.concatenate(blocks, axis=0).astype(BF16)
    sl = t1r.at[r8]
    for k in FAR_FIRST:
        remote(sl, sl, sent.at[G_F], got.at[G_F], at_xc(k)).start()
    all_sent(G_N, ns.at[seven])
    all_got(G_F, t1r.at[seven])
    sums = [jnp.zeros((8, 384), F32) for _ in range(ZN)]
    for source in range(8):
        from_there = t1r[source].astype(F32)
        for c in range(CAP):
            block = from_there[8 * c : 8 * c + 8]
            question = block[:, 260:261]
            for zz in range(ZN):
                here = question == (zz * 8 + r8).astype(F32)
                sums[zz] += jnp.where(here, block, 0.0)
    for zz in range(ZN):
        t2s[zz] = jnp.concatenate([sums[zz], jnp.zeros((8, 384), F32)], axis=0).astype(BF16)
    for k in FAR_FIRST:
        remote(t2s.at[wrap(z + k, ZN)], t2r.at[z], sent.at[G_H], got.at[G_H], at_z(k)).start()
    all_sent(G_F, t1r.at[seven])
    all_got(G_H, t2r.at[seven])
    answer = t2s[z].astype(F32)
    for k in range(1, 8):
        answer += t2r[wrap(z - k, ZN)].astype(F32)
    below = jnp.zeros((8, 256), F32)
    for h in range(4):
        below = jnp.where(lane_head == h, answer[0:8, 256 + h : 257 + h], below)
    out[0] = (answer[0:8, 0:256] / below).astype(BF16)
    all_sent(G_H, t2s.at[seven])


def body(
    question_states, passage_cache, norm_gain, enc_wq, enc_wk, enc_wv, enc_wo, dec_wk, dec_wv, dec_queries,
    passage_ids, location, question_lengths,
):
    vmem = pl.BlockSpec(memory_space=pltpu.VMEM)
    anywhere = pl.BlockSpec(memory_space=pl.ANY)
    dma = pltpu.SemaphoreType.DMA
    return pl.pallas_call(
        kernel,
        name="step",
        out_shape=jax.ShapeDtypeStruct((1, 8, 256), BF16),
        in_specs=[anywhere] * 13,
        out_specs=vmem,
        scratch_shapes=[
            pltpu.SMEM((2, 64), jnp.int32),
            pltpu.SMEM((256,), jnp.int32),
            pltpu.SMEM((64,), jnp.int32),
            pltpu.VMEM((1, 8, 512), BF16),
            pltpu.VMEM((4, 64, 512), BF16),
            pltpu.VMEM((32, 128), F32),
            pltpu.VMEM((1, 8, 256), BF16),
            pltpu.VMEM((2, 32, 64, 768), BF16),
            pltpu.VMEM((64, 64, 256), BF16),
            pltpu.VMEM((64, 256), BF16),
            pltpu.VMEM((8, 240, 512), BF16),
            pltpu.VMEM((64, 16, 384), BF16),
            pltpu.VMEM((224, 4096), BF16),
            pltpu.VMEM((8, 2, 224, 128), BF16),
            pltpu.VMEM((224, 512), BF16),
            pltpu.VMEM((3, 128, 512), BF16),
            pltpu.VMEM((3, 256, 512), BF16),
            pltpu.VMEM((8, 96, 128), BF16),
            pltpu.VMEM((8, 96, 128), BF16),
            pltpu.VMEM((8, 96, 128), BF16),
            pltpu.VMEM((8, 32, 256), BF16),
            pltpu.VMEM((8, 32, 256), BF16),
            pltpu.VMEM((8, 32, 384), BF16),
            pltpu.VMEM((8, 16, 384), BF16),
            pltpu.VMEM((8, 16, 384), BF16),
            pltpu.VMEM((512, 2048), BF16),
            pltpu.VMEM((512, 2048), BF16),
            dma((13,)),
            dma((2, 5)),
            dma((8, 2, 5)),
            dma((1,)),
            dma((2, 5)),
            dma((2, 10)),
            dma((17,)),
            dma((17,)),
        ],
        compiler_params=pltpu.CompilerParams(
            collective_id=0, has_side_effects=True, vmem_limit_bytes=56 * 2**20
        ),
    )(
        passage_ids.T, location, question_lengths, question_states, passage_cache, norm_gain.reshape(32, 128),
        enc_wq, enc_wk, enc_wv, enc_wo.T,
        dec_wk, dec_wv, dec_queries,
    )


def solution(mesh):
    in_specs = (
        P("mem", None, "dec"),
        P("mem", None, "dec"),
        P(),
        P("mem", "dec"),
        P("mem", "dec"),
        P("mem", "dec"),
        P("dec", "mem"),
        P("dec", None),
        P("dec", None),
        P("mem", None, "dec"),
        P(),
        P(),
        P(),
    )
    return jax.shard_map(body, mesh=mesh, in_specs=in_specs, out_specs=P("mem", None, "dec"), check_vma=False)
```
